256 devices in a mesh: ctx: 4 (over z_lo), att: 2 (over core), exp: 32 (over z_hi, x, y).
Axes of the slice: x: 4, y: 4, z: 8 (z_hi: 2, z_lo: 4; z = z_hi * 4 + z_lo), core: 2. Of those that a mesh axis runs over, the one named last changes fastest.
Arguments:
- query_latent: bfloat16 [64, 128, 512], P(('att', 'exp')), may hold values from -8 to 8
- query_rope: bfloat16 [64, 128, 64], P(('att', 'exp')), may hold values from -8 to 8
- latent_cache: bfloat16 [64, 4096, 512], P(('att', 'exp'), 'ctx'), may hold values from -4 to 4
- rope_keys: bfloat16 [64, 64, 4096], P(('att', 'exp'), None, 'ctx'), may hold values from -4 to 4
- lengths: int32 [64], P(('att', 'exp')), may hold values from 256 to 4096, as said below
- moe_rows: bfloat16 [1024, 7168], P(('ctx', 'att', 'exp'))
- route_ids: int32 [1024, 8], P(('ctx', 'att', 'exp')), may hold values from 0 to 31, all different within a row; in each aligned block of 4 rows (0 to 3, 4 to 7, ...) at most 2 rows name the same one
- route_gates: float32 [1024, 8], P(('ctx', 'att', 'exp')), may hold values from 0.05 to 0.5
- norm_gain: bfloat16 [7168], replicated, may hold values from 0.099609375 to 1.8984375
- expert_in: bfloat16 [32, 2, 7168, 2048], P('exp', None, None, ('ctx', 'att')), may hold values from -0.0625 to 0.0625
- expert_out: bfloat16 [32, 2048, 7168], P('exp', None, ('ctx', 'att')), may hold values from -0.125 to 0.125
Outputs:
- attended: bfloat16 [64, 128, 512], P(('att', 'exp'), 'ctx')
- routed_sum: bfloat16 [1024, 7168], P(('ctx', 'att', 'exp'))
The draws below stay inside these ranges and needn't reach their ends.
Inputs may be any that keep to these rules, and one draw needn't show every extreme that they name: `route_ids`: each row names 8 different experts; among the 4 rows of one device no expert is named by more than 2 rows, a bound that some block reaches. `lengths`: some sequence has all 4096 positions live.
All inputs are finite; a program needn't handle non-finite values.
Results may differ from the reference program's by a relative error of at most 0.007.
Values may be sent and summed in bfloat16 or wider, within the bound.
No kernel may reach another device: no remote copies, remote signals or barrier semaphores. Data moves between devices by JAX's collectives and lax.ppermute only.
A program may use at most 64 MiB of HBM per device.

```python
import math
import jax
import jax.numpy as jnp
import numpy as np
from jax import lax

D = 7168
H = 128
R = 512
P_SIZE = 64
FFW = 2048
TOK_DEV = 4
CTX_LEN = 4096
NSEQ = 64
EXPERTS = 32
TOP = 8
CAP = 2
TOKENS = 1024
N_CTX = 4
N_ATT = 2
N_EXP = 32


def draw_lengths(key, part):
    key = jax.random.fold_in(key, 11)
    first_key, second_key = jax.random.split(key)
    drawn_lengths = jax.random.randint(first_key, (NSEQ,), CTX_LEN // 16, CTX_LEN + 1, dtype=jnp.int32)
    ordering = jax.random.permutation(second_key, NSEQ)
    drawn_lengths = drawn_lengths.at[ordering[0]].set(CTX_LEN)
    drawn_lengths = drawn_lengths.at[ordering[1]].set(CTX_LEN // 16)
    return drawn_lengths.astype(jnp.int32)


def draw_moe_rows(key, part):
    key = jax.random.fold_in(key, 23)
    noise_key, row_key, column_key = jax.random.split(key, 3)
    noise_field = jax.random.truncated_normal(noise_key, -4.0, 4.0, (TOKENS, D), jnp.float32)
    spread = math.log(10.0)
    row_scale = jnp.exp(jax.random.uniform(row_key, (TOKENS, 1), jnp.float32, 0.0, spread))
    column_scale = jnp.exp(jax.random.uniform(column_key, (1, D), jnp.float32, 0.0, spread))
    return (noise_field * row_scale * column_scale).astype(jnp.bfloat16)


def steps_of(own_key, shape, shards, low, largest):
    def one(dim, parts):
        draws = jax.random.uniform(jax.random.fold_in(jax.random.fold_in(own_key, 6), dim), (parts,), jnp.float32, low / len(shards), largest / len(shards))
        return jnp.repeat(jnp.exp(draws), shape[dim] // parts).reshape((-1,) + (1,) * (len(shape) - dim - 1))

    level = one(*shards[0])
    for cut in shards[1:]:
        level = level * one(*cut)
    return level


def deal_out(stream_key, own, number, rows, amount, top, bound, skew):
    sequence = jax.random.permutation(stream_key, amount)
    crowded, common = load_shares(amount, rows * top, bound, skew, True), load_shares(amount, rows * top, bound, skew, False)
    places = jnp.arange(amount)

    def named(sizes, rotation):
        used = int((sizes > 0).sum())
        fixed = max(1, used // 4)
        passed = fixed + (places - fixed + rotation * (used - fixed)) % max(1, amount - fixed)
        return jnp.zeros((amount,), jnp.int32).at[sequence[jnp.where(places < fixed, places, passed)]].set(jnp.asarray(sizes, jnp.int32))

    sizes = jnp.where(number % 4 == 0, named(crowded, number // 4), named(common, number - number // 4 - 1))
    mixed = jax.random.permutation(jax.random.fold_in(own, 3), amount)
    source_of, sink = mixed[0:amount // 2 * 2:2], mixed[1:amount // 2 * 2:2]
    room = jnp.minimum(sizes[source_of] - 1, bound - sizes[sink]) // 2
    room = jnp.where((source_of == sequence[0]) | (sink == sequence[0]) | (sizes[sink] == 0), 0, jnp.maximum(room, 0))
    passed = jax.random.randint(jax.random.fold_in(own, 4), (amount // 2,), 0, 1 << 20) % (room + 1)
    sizes = sizes.at[source_of].add(-passed).at[sink].add(passed)
    members = jnp.searchsorted(jnp.cumsum(sizes), jnp.arange(rows * top), side="right").astype(jnp.int32)
    table = members.reshape(top, rows).T
    table = table[jax.random.permutation(jax.random.fold_in(own, 1), rows)]
    rotation = jax.random.randint(jax.random.fold_in(own, 2), (rows, 1), 0, top)
    return jnp.take_along_axis(table, (jnp.arange(top)[None, :] + rotation) % top, axis=1)


def load_shares(count, total, bound, skew, full):
    portions = [(1 << 20) // math.isqrt(rank ** skew) + 1 for rank in range(1, count + 1)]
    largest = bound if full else min(bound, max(-(-total // count), total * portions[0] // sum(portions)))
    least = 1 if total - largest >= count - 1 else 0
    given, surplus = [largest] + [least] * (count - 1), total - largest - least * (count - 1)
    while surplus > 0:
        free = [i for i in range(1, count) if given[i] < largest] or [i for i in range(1, count) if given[i] < bound]
        pool, remaining = sum([portions[i] for i in free]), surplus
        for i in free:
            extra = min(bound - given[i], max(1, remaining * portions[i] // pool), surplus)
            given[i] = given[i] + extra
            surplus = surplus - extra
    return np.array(given)


def centred(own_key, dims, width, most, cuts=(), kind=jnp.bfloat16):
    values = width * jax.random.normal(own_key, dims, jnp.float32)
    if cuts:
        values = values * steps_of(own_key, dims, cuts, -0.22, 0.18)
    return jnp.clip(values, -most, most).astype(kind)


def setup_inputs(seed: int = 0) -> dict:
    splits = jax.random.split(jax.random.key(seed), 12)
    query_latent = centred(splits[0], (NSEQ, H, R), 1.6, 8.0, ((0, 64),))
    query_rope = centred(splits[1], (NSEQ, H, P_SIZE), 1.6, 8.0, ((0, 64),))
    latent_cache = centred(splits[2], (NSEQ, CTX_LEN, R), 1.0, 4.0, ((0, 64), (1, 4)))
    rope_keys = centred(splits[3], (NSEQ, P_SIZE, CTX_LEN), 1.0, 4.0, ((0, 64), (2, 4)))
    lengths = draw_lengths(jax.random.fold_in(splits[11], 71), 0)
    moe_rows = draw_moe_rows(jax.random.fold_in(splits[11], 71), 0)
    route_ids_keys = jax.random.split(jax.random.fold_in(splits[6], 1), TOKENS // TOK_DEV)
    route_ids_turns = jax.random.permutation(jax.random.fold_in(splits[6], 3), TOKENS // TOK_DEV)
    route_ids = jax.vmap(lambda own, number: deal_out(jax.random.fold_in(splits[6], 2), own, number, TOK_DEV, EXPERTS, TOP, CAP, 2))(route_ids_keys, route_ids_turns).reshape((TOKENS, TOP))
    route_gates = jnp.clip(jnp.exp(math.log(0.5) - 2.3025851 * jax.random.uniform(splits[7], (TOKENS, TOP), jnp.float32) ** steps_of(splits[7], (TOKENS, TOP), ((0, 256),), -0.2, 0.2)), 0.05, 0.5)
    norm_gain = jnp.clip(1.0 + 0.18 * jax.random.normal(splits[8], (D,), jnp.float32), 0.099609375, 1.8984375).astype(jnp.bfloat16)
    expert_in = centred(splits[9], (EXPERTS, 2, D, FFW), D ** -0.5, 0.0625, ((0, 32), (3, 8)))
    expert_out = centred(splits[10], (EXPERTS, FFW, D), FFW ** -0.5, 0.125, ((0, 32), (2, 8)))
    return dict(query_latent=query_latent, query_rope=query_rope, latent_cache=latent_cache, rope_keys=rope_keys, lengths=lengths, moe_rows=moe_rows, route_ids=route_ids, route_gates=route_gates, norm_gain=norm_gain, expert_in=expert_in, expert_out=expert_out)


softmax_scale = 192.0 ** (-0.5)
epsilon = 1e-06

def attend_one(packed):
    latent_query, rope_query, cache_rows, key_rows, length_one = packed
    scores = jnp.dot(latent_query, cache_rows.T, preferred_element_type=jnp.float32) + jnp.dot(rope_query, key_rows, preferred_element_type=jnp.float32)
    position = jnp.arange(CTX_LEN, dtype=jnp.int32)
    weights = jnp.where(position[None, :] < length_one, jnp.exp(softmax_scale * scores), jnp.float32(0.0))
    mass = lax.optimization_barrier(jnp.sum(weights, axis=1))
    rounded = weights.astype(jnp.bfloat16)
    numerator = jnp.dot(rounded, cache_rows, preferred_element_type=jnp.float32)
    return (numerator / mass[:, None]).astype(jnp.bfloat16)

def reference(query_latent, query_rope, latent_cache, rope_keys, lengths, moe_rows, route_ids, route_gates, norm_gain, expert_in, expert_out):
    attended = lax.map(attend_one, (query_latent, query_rope, latent_cache, rope_keys, lengths))
    widened = moe_rows.astype(jnp.float32)
    normed = (widened * lax.rsqrt(lax.optimization_barrier(jnp.mean(widened * widened, axis=1, keepdims=True)) + epsilon) * norm_gain.astype(jnp.float32)).astype(jnp.bfloat16)
    expert_ids = jnp.arange(EXPERTS, dtype=jnp.int32)
    picks = route_ids[:, :, None] == expert_ids[None, None, :]
    chosen = jnp.any(picks, axis=1)
    gate_share = lax.optimization_barrier(jnp.sum(jnp.where(picks, route_gates[:, :, None], jnp.float32(0.0)), axis=1))
    kept = min(TOKENS, N_CTX * N_ATT * N_EXP * CAP)

    def one_expert(running, expert):
        member = jnp.take(chosen, expert, axis=1)
        ordering = jnp.argsort(jnp.logical_not(member).astype(jnp.int32), stable=True)[:kept].astype(jnp.int32)
        gathered = jnp.take(normed, ordering, axis=0)
        gate_part = jnp.dot(gathered, expert_in[expert, 0], preferred_element_type=jnp.float32)
        up_part = jnp.dot(gathered, expert_in[expert, 1], preferred_element_type=jnp.float32)
        hidden = (jax.nn.silu(gate_part) * up_part).astype(jnp.bfloat16)
        result = jnp.dot(hidden, expert_out[expert], preferred_element_type=jnp.float32).astype(jnp.bfloat16)
        share = jnp.take(jnp.take(gate_share, ordering, axis=0), expert, axis=1)
        running = running.at[ordering].add(share[:, None] * result.astype(jnp.float32))
        return (running, None)
    accumulated, unused = lax.scan(one_expert, jnp.zeros((TOKENS, D), jnp.float32), expert_ids)
    return (attended, accumulated.astype(jnp.bfloat16))
```

```python
import jax
import jax.numpy as jnp
from jax import lax
from jax.sharding import Mesh, PartitionSpec as P

softmax_scale = 192.0 ** (-0.5)
epsilon = 1e-06
bf16 = jnp.bfloat16
f32 = jnp.float32
INFO = 128
TOK = 4
SLOTS = 2


def attend(query_latent, query_rope, latent_cache, rope_keys, lengths):
    shard_length = latent_cache.shape[1]
    first_position = lax.axis_index("ctx") * shard_length
    scores = jnp.einsum("hr,tr->ht", query_latent[0], latent_cache[0], preferred_element_type=f32)
    scores = scores + jnp.einsum("hp,pt->ht", query_rope[0], rope_keys[0], preferred_element_type=f32)
    position = first_position + jnp.arange(shard_length, dtype=jnp.int32)
    live_mask = position < lengths[0]
    weights = jnp.where(live_mask[None, :], jnp.exp(softmax_scale * scores), f32(0.0))
    mass = jnp.sum(weights, axis=1, keepdims=True)
    numerator = jnp.dot(weights.astype(bf16), latent_cache[0], preferred_element_type=f32)
    return jnp.concatenate([numerator, jnp.broadcast_to(mass, (mass.shape[0], 128))], axis=1)


def finish_attention(summed):
    return (summed[:, :512] / summed[:, 512:513]).astype(bf16)[None]


def split3(values):
    high = lax.reduce_precision(values, 8, 7)
    rest = values - high
    middle = lax.reduce_precision(rest, 8, 7)
    low = rest - middle
    return [high.astype(bf16), middle.astype(bf16), low.astype(bf16)]


def slot_table(ids, z_half):
    experts = (z_half * 16 + jnp.arange(16, dtype=jnp.int32)).astype(f32)
    picks = ids[None] == experts[:, None, None, None]
    chosen = jnp.any(picks, axis=3).astype(f32)
    before = [jnp.zeros_like(chosen[:, :, 0])]
    for t in range(TOK - 1):
        before.append(before[-1] + chosen[:, :, t])
    before = jnp.stack(before, axis=2)
    slot = jnp.arange(SLOTS, dtype=jnp.int32).astype(f32)
    placed = (chosen[..., None] == 1) & (before[..., None] == slot)
    return placed, picks


def shards(
    query_latent,
    query_rope,
    latent_cache,
    rope_keys,
    lengths,
    moe_rows,
    route_ids,
    route_gates,
    norm_gain,
    expert_in,
    expert_out,
):
    c = lax.axis_index("ctx")
    a = lax.axis_index("att")
    h = lax.axis_index("zhi")
    width = moe_rows.shape[1]
    swap_core = [(0, 1), (1, 0)]

    widened = moe_rows.astype(f32)
    normed = (
        widened
        * lax.rsqrt(jnp.mean(widened * widened, axis=1, keepdims=True) + epsilon)
        * norm_gain.astype(f32)
    ).astype(bf16)
    info = jnp.concatenate(
        [route_ids.astype(bf16)] + split3(route_gates) + [jnp.zeros((TOK, INFO - 32), bf16)], axis=1
    )
    payload = jnp.concatenate([normed, info], axis=1)

    def hop(value, k, flip):
        pairs = [
            (i * 2 + j, (i + k) % 4 * 2 + (j ^ flip)) for i in range(4) for j in range(2)
        ]
        return lax.ppermute(value, ("ctx", "zhi"), pairs)

    own_half = [payload] + [hop(payload, k, 0) for k in (1, 2, 3)]
    other_half = [hop(payload, k, 1) for k in (0, 1, 2, 3)]
    origin = (c - jnp.arange(4, dtype=jnp.int32)) % 4
    absolute = origin[None, :] == jnp.arange(4, dtype=jnp.int32)[:, None]

    part = attend(query_latent, query_rope, latent_cache, rope_keys, lengths)
    summed = lax.psum_scatter(part, "ctx", scatter_dimension=0, tiled=True)

    down = expert_out[0].reshape(4, 2, 256, 896)
    down_rel = jnp.concatenate(
        [
            lax.dynamic_slice(down, ((c - k) % 4, jnp.where(r == 0, a, 1 - a), 0, 0), (1, 1, 256, 896)).reshape(256, 896)
            for r in (0, 1)
            for k in range(4)
        ],
        axis=0,
    )

    def dispatch(half):
        tokens = jnp.concatenate(half, axis=0)
        ids = tokens[:, width : width + 8].astype(f32).reshape(4, TOK, 8)
        placed, _ = slot_table(ids, h)
        selector = placed.transpose(0, 3, 1, 2)[:, None] & absolute[None, :, None, :, None]
        selector = selector.astype(bf16).reshape(16 * 4 * SLOTS, 4 * TOK)
        rows = jnp.dot(selector, tokens[:, :width], preferred_element_type=f32).astype(bf16)
        rows = rows.reshape(16, 4 * SLOTS, width)
        got = lax.all_to_all(rows, ("x", "y"), split_axis=0, concat_axis=0, tiled=True)
        return got.reshape(128, width)

    def experts_of(got):
        other = lax.ppermute(got, "att", swap_core)
        rows = jnp.concatenate([got, other], axis=0)
        gate = jnp.dot(rows, expert_in[0, 0], preferred_element_type=f32)
        up = jnp.dot(rows, expert_in[0, 1], preferred_element_type=f32)
        hidden = (jax.nn.silu(gate) * up).astype(bf16)
        pieces = [hidden] + [hop(hidden, k, 0) for k in (1, 2, 3)]
        mine = jnp.concatenate(pieces, axis=1)
        theirs = lax.ppermute(mine, "att", swap_core)
        theirs = jnp.concatenate([theirs[128:], theirs[:128]], axis=0)
        result = jnp.dot(
            jnp.concatenate([mine, theirs], axis=1), down_rel, preferred_element_type=f32
        ).astype(bf16)
        result = result.reshape(2, 16, 8, 896).transpose(1, 0, 2, 3)
        return lax.all_to_all(result, ("x", "y"), split_axis=0, concat_axis=0, tiled=True)

    def mix(half, back):
        mine = jnp.concatenate([v[:, width:] for v in half], axis=0)
        theirs = lax.ppermute(mine, "att", swap_core)
        total = []
        for r, facts in enumerate((mine, theirs)):
            facts = facts.astype(f32).reshape(4, TOK, INFO)
            facts = jnp.sum(jnp.where(absolute[:, :, None, None], facts[None], f32(0.0)), axis=1)
            placed, picks = slot_table(facts[:, :, :8], h)
            gates = facts[:, :, 8:16] + facts[:, :, 16:24] + facts[:, :, 24:32]
            share = jnp.sum(jnp.where(picks, gates[None], f32(0.0)), axis=3)
            weight = jnp.where(placed, share[..., None], f32(0.0)).transpose(1, 2, 0, 3)
            same = jnp.eye(4, dtype=jnp.bool_)
            matrix = jnp.where(same[:, None, None, :, None], weight[:, :, :, None, :], f32(0.0))
            matrix = matrix.reshape(4 * TOK, 16 * 4 * SLOTS)
            total.append(
                jnp.dot(
                    matrix,
                    back[:, r].reshape(16 * 8, 896).astype(f32),
                    precision=lax.Precision.HIGHEST,
                ).reshape(4, TOK, 896)
            )
        first = jnp.where(a == 0, total[0], total[1])
        second = jnp.where(a == 0, total[1], total[0])
        return jnp.stack([first, second], axis=1)

    got_own = dispatch(own_half)
    got_other = dispatch(other_half)
    mixed_own = mix(own_half, experts_of(got_own))
    mixed_other = mix(other_half, experts_of(got_other))
    first = jnp.where(h == 0, mixed_own, mixed_other)
    second = jnp.where(h == 0, mixed_other, mixed_own)
    outgoing = jnp.stack([first, second], axis=2).astype(bf16)
    final = lax.all_to_all(
        outgoing.reshape(16, TOK, 896), ("ctx", "att", "zhi"), split_axis=0, concat_axis=0, tiled=True
    )
    final = final.reshape(8, 2, TOK, 896).astype(f32)
    routed = (final[:, 0] + final[:, 1]).transpose(1, 0, 2).reshape(TOK, 8 * 896)
    return (finish_attention(summed), routed.astype(bf16))


def solution(mesh):
    fine = Mesh(mesh.devices.reshape(4, 2, 2, 4, 4), ("ctx", "att", "zhi", "x", "y"))
    exp = ("zhi", "x", "y")
    sequences = ("att",) + exp
    every = ("ctx", "att") + exp
    placed = (
        P(sequences, None, None),
        P(sequences, None, None),
        P(sequences, "ctx", None),
        P(sequences, None, "ctx"),
        P(sequences),
        P(every, None),
        P(every, None),
        P(every, None),
        P(),
        P(exp, None, None, ("ctx", "att")),
        P(exp, None, ("ctx", "att")),
    )
    return jax.shard_map(
        shards,
        mesh=fine,
        in_specs=placed,
        out_specs=(P(sequences, "ctx", None), P(every, None)),
        check_vma=False,
    )
```

```python
import jax
import jax.numpy as jnp
from jax import lax
from jax.experimental import pallas as pl
from jax.experimental.pallas import tpu as pltpu
from jax.sharding import Mesh, PartitionSpec as P

softmax_scale = 192.0 ** (-0.5)
epsilon = 1e-06
bf16 = jnp.bfloat16
f32 = jnp.float32
INFO = 128
TOK = 4
SLOTS = 2


def attend(query_latent, query_rope, latent_cache, rope_keys, lengths):
    shard_length = latent_cache.shape[1]
    first_position = lax.axis_index("ctx") * shard_length
    scores = jnp.einsum("hr,tr->ht", query_latent[0], latent_cache[0], preferred_element_type=f32)
    scores = scores + jnp.einsum("hp,pt->ht", query_rope[0], rope_keys[0], preferred_element_type=f32)
    position = first_position + jnp.arange(shard_length, dtype=jnp.int32)
    live_mask = position < lengths[0]
    weights = jnp.where(live_mask[None, :], jnp.exp(softmax_scale * scores), f32(0.0))
    mass = jnp.sum(weights, axis=1, keepdims=True)
    numerator = jnp.dot(weights.astype(bf16), latent_cache[0], preferred_element_type=f32)
    return jnp.concatenate([numerator, jnp.broadcast_to(mass, (mass.shape[0], 128))], axis=1)


def finish_attention(summed):
    return (summed[:, :512] / summed[:, 512:513]).astype(bf16)[None]


VMEM = pl.BlockSpec(memory_space=pltpu.VMEM)
SMEM = pl.BlockSpec(memory_space=pltpu.SMEM)
ROOM = pltpu.CompilerParams(vmem_limit_bytes=40 * 1024 * 1024)


def prepare_kernel(ids_ref, gates_ref, rows_ref, gain_ref, out_ref):
    width = rows_ref.shape[1]
    rows = rows_ref[...].astype(f32)
    mean = jnp.mean(rows * rows, axis=1, keepdims=True)
    gain = gain_ref[...].astype(f32).reshape(1, width)
    out_ref[:, :width] = (rows * lax.rsqrt(mean + epsilon) * gain).astype(bf16)
    lane = lax.broadcasted_iota(jnp.int32, (1, 128), 1)
    expert, slot = lane // SLOTS, lane % SLOTS
    count = jnp.zeros((1, 128), jnp.int32)
    token = jnp.full((1, 128), -1.0, f32)
    gate = jnp.zeros((1, 128), f32)
    for t in range(TOK):
        picked = jnp.zeros((1, 128), jnp.int32)
        share = jnp.zeros((1, 128), f32)
        for j in range(8):
            hit = expert == ids_ref[t, j]
            picked = jnp.where(hit, 1, picked)
            share = share + jnp.where(hit, gates_ref[t, j], f32(0.0))
        here = (picked == 1) & (count == slot)
        token = jnp.where(here, f32(t), token)
        gate = jnp.where(here, share, gate)
        count = count + picked
    high = gate.astype(bf16).astype(f32)
    middle = (gate - high).astype(bf16).astype(f32)
    low = gate - high - middle
    row = lax.broadcasted_iota(jnp.int32, (TOK, 128), 0)
    facts = jnp.where(row == 0, token, jnp.where(row == 1, high, jnp.where(row == 2, middle, low)))
    out_ref[:, width:] = facts.astype(bf16)


def prepare(moe_rows, route_ids, route_gates, norm_gain):
    return pl.pallas_call(
        prepare_kernel,
        out_shape=jax.ShapeDtypeStruct((TOK, moe_rows.shape[1] + INFO), bf16),
        in_specs=[SMEM, SMEM, VMEM, VMEM],
        out_specs=VMEM,
    )(route_ids, route_gates, moe_rows, norm_gain)


def gate_up_kernel(place_ref, own_ref, other_ref, weight_ref, out_ref):
    rows = jnp.concatenate([own_ref[...], other_ref[...]], axis=0)
    gate = jnp.dot(rows, weight_ref[0], preferred_element_type=f32)
    up = jnp.dot(rows, weight_ref[1], preferred_element_type=f32)
    hidden = gate / (1.0 + jnp.exp(-gate)) * up
    own, other = hidden[:128], hidden[128:]
    core = place_ref[1]
    first = jnp.where(core == 0, own, other).reshape(16, 8, 256)
    second = jnp.where(core == 0, other, own).reshape(16, 8, 256)
    out_ref[...] = jnp.concatenate([first, second], axis=1).reshape(256, 256).astype(bf16)


def gate_up(place, own, other, weight):
    width = own.shape[1]
    return pl.pallas_call(
        gate_up_kernel,
        out_shape=jax.ShapeDtypeStruct((256, 256), bf16),
        in_specs=[SMEM, VMEM, VMEM, VMEM],
        out_specs=VMEM,
        compiler_params=ROOM,
        cost_estimate=pl.CostEstimate(
            flops=2 * 256 * width * 512, bytes_accessed=2 * width * (512 + 256), transcendentals=65536
        ),
    )(place, own, other, weight)


def down_kernel(place_ref, p0, p1, p2, p3, theirs_ref, weight_ref, out_ref):
    ctx, core = place_ref[0], place_ref[1]
    total = jnp.zeros(out_ref.shape, f32)
    for k, piece in enumerate((p0, p1, p2, p3)):
        source = (ctx - k + 4) % 4
        total += jnp.dot(piece[...], weight_ref[source, core], preferred_element_type=f32)
        theirs = theirs_ref[:, k * 256 : (k + 1) * 256]
        total += jnp.dot(theirs, weight_ref[source, 1 - core], preferred_element_type=f32)
    out_ref[...] = total.astype(bf16)


def down(place, pieces, theirs, weight):
    return pl.pallas_call(
        down_kernel,
        out_shape=jax.ShapeDtypeStruct((256, 896), bf16),
        in_specs=[SMEM] + [VMEM] * 6,
        out_specs=VMEM,
        compiler_params=ROOM,
        cost_estimate=pl.CostEstimate(
            flops=2 * 256 * 2048 * 896, bytes_accessed=2 * 2048 * 896 + 2 * 256 * 2048, transcendentals=0
        ),
    )(place, *pieces, theirs, weight)


def mix_kernel(place_ref, back0, back1, mine0, mine1, theirs0, theirs1, out_ref):
    ctx, core, half = place_ref[0], place_ref[1], place_ref[2]

    def grid(rows, columns, dim):
        return lax.broadcasted_iota(jnp.int32, (rows, columns), dim)

    def lanes(rows):
        at = grid(rows, 256, 1)
        return at // 16, at // 8 % 2, at // 2 % 4, at % 2

    expert, _, _, slot = lanes(128)
    spread = (grid(128, 256, 0) == half * 32 + expert * SLOTS + slot).astype(f32).astype(bf16)
    total = jnp.zeros(out_ref.shape, f32)
    for q, (back, mine, theirs) in enumerate(((back0, mine0, theirs0), (back1, mine1, theirs1))):
        facts = jnp.concatenate([mine[...], theirs[...]], axis=0)
        facts = jnp.dot(facts, spread, preferred_element_type=f32)
        at = grid(32, 256, 0)
        _, lane_core, lane_ctx, _ = lanes(32)
        source_core = jnp.where(at // 16 == 0, core, 1 - core)
        here = (source_core == lane_core) & ((ctx - at // 4 % 4 + 4) % 4 == lane_ctx)
        token, high, middle, low = (
            jnp.sum(jnp.where(here & (at % 4 == i), facts, 0.0), axis=0, keepdims=True) for i in range(4)
        )
        _, lane_core, lane_ctx, _ = lanes(64)
        at = grid(64, 256, 0)
        fits = (at // 16 == lane_ctx) & (at // 8 % 2 == lane_core)
        fits = fits & (at // 4 % 2 == (half if q == 0 else 1 - half))
        fits = fits & ((at % 4).astype(f32) == token)
        for part in (high, middle, low):
            matrix = jnp.where(fits, part, 0.0).astype(bf16)
            total += jnp.dot(matrix, back[...], preferred_element_type=f32)
    out_ref[...] = total.astype(bf16)


def mix(place, back0, back1, mine0, mine1, theirs0, theirs1):
    return pl.pallas_call(
        mix_kernel,
        out_shape=jax.ShapeDtypeStruct((64, 896), bf16),
        in_specs=[SMEM] + [VMEM] * 6,
        out_specs=VMEM,
        cost_estimate=pl.CostEstimate(flops=2 * 64 * 512 * 896 * 3, bytes_accessed=1 << 20, transcendentals=0),
    )(place, back0, back1, mine0, mine1, theirs0, theirs1)


def shards(
    query_latent,
    query_rope,
    latent_cache,
    rope_keys,
    lengths,
    moe_rows,
    route_ids,
    route_gates,
    norm_gain,
    expert_in,
    expert_out,
):
    c = lax.axis_index("ctx")
    a = lax.axis_index("att")
    h = lax.axis_index("zhi")
    width = moe_rows.shape[1]
    swap_core = [(0, 1), (1, 0)]

    place = jnp.stack([c, a, h]).astype(jnp.int32)
    payload = prepare(moe_rows, route_ids, route_gates, norm_gain)

    def hop(value, k, flip):
        pairs = [
            (i * 2 + j, (i + k) % 4 * 2 + (j ^ flip)) for i in range(4) for j in range(2)
        ]
        return lax.ppermute(value, ("ctx", "zhi"), pairs)

    origin = (c - jnp.arange(4, dtype=jnp.int32)) % 4
    absolute = origin[None, :] == jnp.arange(4, dtype=jnp.int32)[:, None]
    gate_up_weight = expert_in[0]
    down_weight = expert_out[0].reshape(4, 2, 256, 896)

    def choose(half):
        tokens = jnp.concatenate(half, axis=0)
        facts = tokens[:, width:]
        wanted = facts.reshape(4, TOK, INFO)[:, 0].astype(f32)
        wanted = jnp.where(h == 0, wanted[:, :32], wanted[:, 32:64]).reshape(4, 16, SLOTS)
        number = jnp.arange(TOK, dtype=jnp.int32).astype(f32)
        hit = wanted.transpose(1, 2, 0)[:, None, :, :, None] == number
        selector = (hit & absolute[None, :, None, :, None]).astype(bf16).reshape(128, 4 * TOK)
        rows = jnp.dot(selector, tokens[:, :width], preferred_element_type=f32).astype(bf16)
        return rows.reshape(16, 4 * SLOTS, width), facts

    def across(value):
        return lax.all_to_all(value, ("x", "y"), split_axis=0, concat_axis=0, tiled=True)

    def hidden_of(got):
        got = got.reshape(128, width)
        hidden = gate_up(place, got, lax.ppermute(got, "att", swap_core), gate_up_weight)
        return [hidden] + [hop(hidden, k, 0) for k in (1, 2, 3)]

    def down_of(pieces, joined):
        theirs = lax.ppermute(joined, "att", swap_core)
        return down(place, pieces, theirs, down_weight).reshape(16, 16, 896)

    rows0, facts0 = choose([payload] + [hop(payload, k, 0) for k in (1, 2, 3)])
    rows0, facts0, payload = lax.optimization_barrier((rows0, facts0, payload))
    got0 = across(rows0)
    rows1, facts1 = choose([hop(payload, k, 1) for k in (0, 1, 2, 3)])
    rows1, facts1, got0 = lax.optimization_barrier((rows1, facts1, got0))
    got1 = across(rows1)

    pieces0 = hidden_of(got0)
    theirs0 = lax.ppermute(facts0, "att", swap_core)
    theirs1 = lax.ppermute(facts1, "att", swap_core)
    part = attend(query_latent, query_rope, latent_cache, rope_keys, lengths)
    result0 = down_of(pieces0, jnp.concatenate(pieces0, axis=1))
    got1, result0, part, theirs0, theirs1 = lax.optimization_barrier((got1, result0, part, theirs0, theirs1))
    summed = lax.psum_scatter(part, "ctx", scatter_dimension=0, tiled=True)
    back0 = across(result0)
    pieces1 = hidden_of(got1)
    joined1, back0 = lax.optimization_barrier((jnp.concatenate(pieces1, axis=1), back0))
    result1 = down_of(pieces1, joined1)
    back1 = across(result1)

    outgoing = mix(place, back0.reshape(256, 896), back1.reshape(256, 896), facts0, facts1, theirs0, theirs1)
    final = lax.all_to_all(
        outgoing.reshape(16, TOK, 896), ("ctx", "att", "zhi"), split_axis=0, concat_axis=0, tiled=True
    )
    final = final.reshape(8, 2, TOK, 896).astype(f32)
    routed = (final[:, 0] + final[:, 1]).transpose(1, 0, 2).reshape(TOK, 8 * 896)
    return (finish_attention(summed), routed.astype(bf16))


def solution(mesh):
    fine = Mesh(mesh.devices.reshape(4, 2, 2, 4, 4), ("ctx", "att", "zhi", "x", "y"))
    exp = ("zhi", "x", "y")
    sequences = ("att",) + exp
    every = ("ctx", "att") + exp
    placed = (
        P(sequences, None, None),
        P(sequences, None, None),
        P(sequences, "ctx", None),
        P(sequences, None, "ctx"),
        P(sequences),
        P(every, None),
        P(every, None),
        P(every, None),
        P(),
        P(exp, None, None, ("ctx", "att")),
        P(exp, None, ("ctx", "att")),
    )
    return jax.shard_map(
        shards,
        mesh=fine,
        in_specs=placed,
        out_specs=(P(sequences, "ctx", None), P(every, None)),
        check_vma=False,
    )
```

```python
import jax
import jax.numpy as jnp
from jax import lax
from jax.experimental import pallas as pl
from jax.experimental.pallas import tpu as pltpu
from jax.sharding import Mesh, PartitionSpec as P

softmax_scale = 192.0 ** (-0.5)
epsilon = 1e-06
bf16 = jnp.bfloat16
f32 = jnp.float32
INFO = 128
TOK = 4
SLOTS = 2


def attend(query_latent, query_rope, latent_cache, rope_keys, lengths):
    shard_length = latent_cache.shape[1]
    first_position = lax.axis_index("ctx") * shard_length
    scores = jnp.einsum("hr,tr->ht", query_latent[0], latent_cache[0], preferred_element_type=f32)
    scores = scores + jnp.einsum("hp,pt->ht", query_rope[0], rope_keys[0], preferred_element_type=f32)
    position = first_position + jnp.arange(shard_length, dtype=jnp.int32)
    live_mask = position < lengths[0]
    weights = jnp.where(live_mask[None, :], jnp.exp(softmax_scale * scores), f32(0.0))
    mass = jnp.sum(weights, axis=1, keepdims=True)
    numerator = jnp.dot(weights.astype(bf16), latent_cache[0], preferred_element_type=f32)
    return jnp.concatenate([numerator, jnp.broadcast_to(mass, (mass.shape[0], 128))], axis=1)


def finish_attention(summed):
    return (summed[:, :512] / summed[:, 512:513]).astype(bf16)[None]


VMEM = pl.BlockSpec(memory_space=pltpu.VMEM)
SMEM = pl.BlockSpec(memory_space=pltpu.SMEM)
ANY = pl.BlockSpec(memory_space=pl.ANY)
CUTS = (0, 1024, 3072, 7168)


def room(mib):
    return pltpu.CompilerParams(vmem_limit_bytes=mib * 1024 * 1024)


def prepare_kernel(ids_ref, gates_ref, rows_ref, gain_ref, out_ref):
    width = rows_ref.shape[1]
    rows = rows_ref[...].astype(f32)
    mean = jnp.mean(rows * rows, axis=1, keepdims=True)
    gain = gain_ref[...].astype(f32).reshape(1, width)
    out_ref[:, :width] = (rows * lax.rsqrt(mean + epsilon) * gain).astype(bf16)
    lane = lax.broadcasted_iota(jnp.int32, (1, 128), 1)
    expert, slot = lane // SLOTS, lane % SLOTS
    count = jnp.zeros((1, 128), jnp.int32)
    token = jnp.full((1, 128), -1.0, f32)
    gate = jnp.zeros((1, 128), f32)
    for t in range(TOK):
        picked = jnp.zeros((1, 128), jnp.int32)
        share = jnp.zeros((1, 128), f32)
        for j in range(8):
            hit = expert == ids_ref[t, j]
            picked = jnp.where(hit, 1, picked)
            share = share + jnp.where(hit, gates_ref[t, j], f32(0.0))
        here = (picked == 1) & (count == slot)
        token = jnp.where(here, f32(t), token)
        gate = jnp.where(here, share, gate)
        count = count + picked
    high = gate.astype(bf16).astype(f32)
    middle = (gate - high).astype(bf16).astype(f32)
    low = gate - high - middle
    row = lax.broadcasted_iota(jnp.int32, (TOK, 128), 0)
    facts = jnp.where(row == 0, token, jnp.where(row == 1, high, jnp.where(row == 2, middle, low)))
    out_ref[:, width:] = facts.astype(bf16)


def prepare(moe_rows, route_ids, route_gates, norm_gain):
    return pl.pallas_call(
        prepare_kernel,
        out_shape=jax.ShapeDtypeStruct((TOK, moe_rows.shape[1] + INFO), bf16),
        in_specs=[SMEM, SMEM, VMEM, VMEM],
        out_specs=VMEM,
        compiler_params=room(4),
    )(route_ids, route_gates, moe_rows, norm_gain)


def choose_kernel(place_ref, facts_ref, tokens_ref, out_ref, selector_ref):
    @pl.when(pl.program_id(0) == 0)
    def _():
        ctx, half = place_ref[0], place_ref[2]

        def grid(rows, columns, dim):
            return lax.broadcasted_iota(jnp.int32, (rows, columns), dim)

        first = grid(16, 16, 1) == grid(16, 16, 0) // TOK * TOK
        tokens = jnp.dot(first.astype(f32).astype(bf16), facts_ref[...], preferred_element_type=f32)
        row = grid(128, 128, 0)
        lane = half * 32 + row // 8 * SLOTS + row % SLOTS
        pick = (grid(128, 128, 1) == lane).astype(f32).astype(bf16)
        wanted = lax.dot_general(
            pick, tokens.astype(bf16), (((1,), (1,)), ((), ())), preferred_element_type=f32
        )
        row, column = grid(128, 16, 0), grid(128, 16, 1)
        hit = wanted == (column % TOK).astype(f32)
        hit = hit & ((ctx - column // TOK + 4) % 4 == row // SLOTS % 4)
        selector_ref[...] = hit.astype(f32).astype(bf16)

    out_ref[...] = jnp.dot(
        selector_ref[...], tokens_ref[...], preferred_element_type=f32
    ).astype(bf16)


def choose(place, tokens, width):
    block = 1024
    return pl.pallas_call(
        choose_kernel,
        out_shape=jax.ShapeDtypeStruct((128, width), bf16),
        grid=(width // block,),
        in_specs=[
            SMEM,
            pl.BlockSpec((4 * TOK, INFO), lambda k: (0, width // INFO)),
            pl.BlockSpec((4 * TOK, block), lambda k: (0, k)),
        ],
        out_specs=pl.BlockSpec((128, block), lambda k: (0, k)),
        scratch_shapes=[pltpu.VMEM((128, 4 * TOK), bf16)],
        compiler_params=room(6),
        cost_estimate=pl.CostEstimate(flops=2 * 128 * 16 * width, bytes_accessed=2 * 144 * width, transcendentals=0),
    )(place, tokens, tokens)


def gate_up_kernel(place_ref, own_ref, other_ref, weight_ref, out_ref, held_ref, sems):
    copies = []
    for i, (low, high) in enumerate(zip(CUTS[:-1], CUTS[1:])):
        part = pl.ds(low, high - low)
        copies.append(pltpu.make_async_copy(weight_ref.at[:, part], held_ref.at[:, part], sems.at[i]))
        copies[-1].start()
    gate = jnp.zeros((256, 256), f32)
    up = jnp.zeros((256, 256), f32)
    for copy, low, high in zip(copies, CUTS[:-1], CUTS[1:]):
        rows = jnp.concatenate([own_ref[:, low:high], other_ref[:, low:high]], axis=0)
        copy.wait()
        gate += jnp.dot(rows, held_ref[0, low:high], preferred_element_type=f32)
        up += jnp.dot(rows, held_ref[1, low:high], preferred_element_type=f32)
    hidden = gate / (1.0 + jnp.exp(-gate)) * up
    own, other = hidden[:128], hidden[128:]
    core = place_ref[1]
    first = jnp.where(core == 0, own, other).reshape(16, 8, 256)
    second = jnp.where(core == 0, other, own).reshape(16, 8, 256)
    out_ref[...] = jnp.concatenate([first, second], axis=1).reshape(256, 256).astype(bf16)


def gate_up(place, own, other, weight):
    width = own.shape[1]
    return pl.pallas_call(
        gate_up_kernel,
        out_shape=jax.ShapeDtypeStruct((256, 256), bf16),
        in_specs=[SMEM, VMEM, VMEM, ANY],
        out_specs=VMEM,
        scratch_shapes=[pltpu.VMEM((2, width, 256), bf16), pltpu.SemaphoreType.DMA((len(CUTS) - 1,))],
        compiler_params=room(16),
        cost_estimate=pl.CostEstimate(
            flops=2 * 256 * width * 512, bytes_accessed=2 * width * (512 + 256), transcendentals=65536
        ),
    )(place, own, other, weight)


def down_kernel(place_ref, p0, p1, p2, p3, theirs_ref, weight_ref, out_ref, held_ref, sems):
    ctx, core = place_ref[0], place_ref[1]
    copies = []
    for k in range(4):
        source = (ctx - k + 4) % 4
        copies.append(pltpu.make_async_copy(weight_ref.at[source], held_ref.at[k], sems.at[k]))
        copies[-1].start()
    total = jnp.zeros(out_ref.shape, f32)
    for k, piece in enumerate((p0, p1, p2, p3)):
        copies[k].wait()
        total += jnp.dot(piece[...], held_ref[k, core], preferred_element_type=f32)
        theirs = theirs_ref[:, k * 256 : (k + 1) * 256]
        total += jnp.dot(theirs, held_ref[k, 1 - core], preferred_element_type=f32)
    out_ref[...] = total.astype(bf16)


def down(place, pieces, theirs, weight):
    return pl.pallas_call(
        down_kernel,
        out_shape=jax.ShapeDtypeStruct((256, 896), bf16),
        in_specs=[SMEM] + [VMEM] * 5 + [ANY],
        out_specs=VMEM,
        scratch_shapes=[pltpu.VMEM((4, 2, 256, 896), bf16), pltpu.SemaphoreType.DMA((4,))],
        compiler_params=room(10),
        cost_estimate=pl.CostEstimate(
            flops=2 * 256 * 2048 * 896, bytes_accessed=2 * 2048 * 896 + 2 * 256 * 2048, transcendentals=0
        ),
    )(place, *pieces, theirs, weight)


def mix_kernel(place_ref, back0, back1, mine0, mine1, theirs0, theirs1, out_ref):
    ctx, core, half = place_ref[0], place_ref[1], place_ref[2]

    def grid(rows, columns, dim):
        return lax.broadcasted_iota(jnp.int32, (rows, columns), dim)

    def lanes(rows):
        at = grid(rows, 256, 1)
        return at // 16, at // 8 % 2, at // 2 % 4, at % 2

    expert, _, _, slot = lanes(128)
    spread = (grid(128, 256, 0) == half * 32 + expert * SLOTS + slot).astype(f32).astype(bf16)
    total = jnp.zeros((64, 896), f32)
    for q, (back, mine, theirs) in enumerate(((back0, mine0, theirs0), (back1, mine1, theirs1))):
        facts = jnp.concatenate([mine[...], theirs[...]], axis=0)
        facts = jnp.dot(facts, spread, preferred_element_type=f32)
        at = grid(32, 256, 0)
        _, lane_core, lane_ctx, _ = lanes(32)
        source_core = jnp.where(at // 16 == 0, core, 1 - core)
        here = (source_core == lane_core) & ((ctx - at // 4 % 4 + 4) % 4 == lane_ctx)
        token, high, middle, low = (
            jnp.sum(jnp.where(here & (at % 4 == i), facts, 0.0), axis=0, keepdims=True) for i in range(4)
        )
        _, lane_core, lane_ctx, _ = lanes(64)
        at = grid(64, 256, 0)
        fits = (at // 16 == lane_ctx) & (at // 8 % 2 == lane_core)
        fits = fits & (at // 4 % 2 == (half if q == 0 else 1 - half))
        fits = fits & ((at % 4).astype(f32) == token)
        for part in (high, middle, low):
            matrix = jnp.where(fits, part, 0.0).astype(bf16)
            total += jnp.dot(matrix, back[...], preferred_element_type=f32)
    out_ref[...] = total.reshape(16, TOK, 896).astype(bf16)


def mix(place, back0, back1, mine0, mine1, theirs0, theirs1):
    return pl.pallas_call(
        mix_kernel,
        out_shape=jax.ShapeDtypeStruct((16, TOK, 896), bf16),
        in_specs=[SMEM] + [VMEM] * 6,
        out_specs=VMEM,
        compiler_params=room(6),
        cost_estimate=pl.CostEstimate(flops=2 * 64 * 512 * 896 * 3, bytes_accessed=1 << 20, transcendentals=0),
    )(place, back0, back1, mine0, mine1, theirs0, theirs1)


def shards(
    query_latent,
    query_rope,
    latent_cache,
    rope_keys,
    lengths,
    moe_rows,
    route_ids,
    route_gates,
    norm_gain,
    expert_in,
    expert_out,
):
    c = lax.axis_index("ctx")
    a = lax.axis_index("att")
    h = lax.axis_index("zhi")
    width = moe_rows.shape[1]
    swap_core = [(0, 1), (1, 0)]

    place = jnp.stack([c, a, h]).astype(jnp.int32)
    payload = prepare(moe_rows, route_ids, route_gates, norm_gain)

    def hop(value, k, flip):
        pairs = [
            (i * 2 + j, (i + k) % 4 * 2 + (j ^ flip)) for i in range(4) for j in range(2)
        ]
        return lax.ppermute(value, ("ctx", "zhi"), pairs)

    gate_up_weight = expert_in[0]
    down_weight = expert_out[0].reshape(4, 2, 256, 896)

    def rows_of(half):
        tokens = jnp.concatenate(half, axis=0)
        rows = choose(place, tokens, width)
        return rows.reshape(16, 4 * SLOTS, width), tokens[:, width:]

    def across(value):
        return lax.all_to_all(value, ("x", "y"), split_axis=0, concat_axis=0, tiled=True)

    def hidden_of(got):
        got = got.reshape(128, width)
        hidden = gate_up(place, got, lax.ppermute(got, "att", swap_core), gate_up_weight)
        return [hidden] + [hop(hidden, k, 0) for k in (1, 2, 3)]

    def down_of(pieces, joined):
        theirs = lax.ppermute(joined, "att", swap_core)
        return down(place, pieces, theirs, down_weight).reshape(16, 16, 896)

    rows0, facts0 = rows_of([payload] + [hop(payload, k, 0) for k in (1, 2, 3)])
    rows0, facts0, payload = lax.optimization_barrier((rows0, facts0, payload))
    got0 = across(rows0)
    rows1, facts1 = rows_of([hop(payload, k, 1) for k in (0, 1, 2, 3)])
    part = attend(query_latent, query_rope, latent_cache, rope_keys, lengths)
    rows1, facts1, got0, part = lax.optimization_barrier((rows1, facts1, got0, part))
    summed = lax.psum_scatter(part, "ctx", scatter_dimension=0, tiled=True)
    got1 = across(rows1)

    pieces0 = hidden_of(got0)
    theirs0 = lax.ppermute(facts0, "att", swap_core)
    theirs1 = lax.ppermute(facts1, "att", swap_core)
    result0 = down_of(pieces0, jnp.concatenate(pieces0, axis=1))
    got1, result0, theirs0, theirs1 = lax.optimization_barrier((got1, result0, theirs0, theirs1))
    back0 = across(result0)
    pieces1 = hidden_of(got1)
    joined1, back0 = lax.optimization_barrier((jnp.concatenate(pieces1, axis=1), back0))
    result1 = down_of(pieces1, joined1)
    back1 = across(result1)

    outgoing = mix(place, back0.reshape(256, 896), back1.reshape(256, 896), facts0, facts1, theirs0, theirs1)
    outgoing, summed = lax.optimization_barrier((outgoing, summed))
    final = lax.all_to_all(
        outgoing, ("ctx", "att", "zhi"), split_axis=0, concat_axis=0, tiled=True
    )
    final = final.reshape(8, 2, TOK, 896).astype(f32)
    routed = (final[:, 0] + final[:, 1]).transpose(1, 0, 2).reshape(TOK, 8 * 896)
    return (finish_attention(summed), routed.astype(bf16))


def solution(mesh):
    fine = Mesh(mesh.devices.reshape(4, 2, 2, 4, 4), ("ctx", "att", "zhi", "x", "y"))
    exp = ("zhi", "x", "y")
    sequences = ("att",) + exp
    every = ("ctx", "att") + exp
    placed = (
        P(sequences, None, None),
        P(sequences, None, None),
        P(sequences, "ctx", None),
        P(sequences, None, "ctx"),
        P(sequences),
        P(every, None),
        P(every, None),
        P(every, None),
        P(),
        P(exp, None, None, ("ctx", "att")),
        P(exp, None, ("ctx", "att")),
    )
    return jax.shard_map(
        shards,
        mesh=fine,
        in_specs=placed,
        out_specs=(P(sequences, "ctx", None), P(every, None)),
        check_vma=False,
    )
```

```python
import jax
import jax.numpy as jnp
from jax import lax
from jax.experimental import pallas as pl
from jax.experimental.pallas import tpu as pltpu
from jax.sharding import Mesh, PartitionSpec as P

softmax_scale = 192.0 ** (-0.5)
epsilon = 1e-06
bf16 = jnp.bfloat16
f32 = jnp.float32
INFO = 128
TOK = 4
SLOTS = 2


def attend(query_latent, query_rope, latent_cache, rope_keys, lengths):
    shard_length = latent_cache.shape[1]
    first_position = lax.axis_index("ctx") * shard_length
    scores = jnp.einsum("hr,tr->ht", query_latent[0], latent_cache[0], preferred_element_type=f32)
    scores = scores + jnp.einsum("hp,pt->ht", query_rope[0], rope_keys[0], preferred_element_type=f32)
    position = first_position + jnp.arange(shard_length, dtype=jnp.int32)
    live_mask = position < lengths[0]
    weights = jnp.where(live_mask[None, :], jnp.exp(softmax_scale * scores), f32(0.0))
    mass = jnp.sum(weights, axis=1, keepdims=True)
    numerator = jnp.dot(weights.astype(bf16), latent_cache[0], preferred_element_type=f32)
    return jnp.concatenate([numerator, jnp.broadcast_to(mass, (mass.shape[0], 128))], axis=1)


def finish_attention(summed):
    return (summed[:, :512] / summed[:, 512:513]).astype(bf16)[None]


VMEM = pl.BlockSpec(memory_space=pltpu.VMEM)
SMEM = pl.BlockSpec(memory_space=pltpu.SMEM)
HBM = pl.BlockSpec(memory_space=pltpu.HBM)
STEP = 1024


def room(mib):
    return pltpu.CompilerParams(vmem_limit_bytes=mib * 1024 * 1024)


def prepare_kernel(ids_ref, gates_ref, rows_ref, gain_ref, out_ref):
    width = rows_ref.shape[1]
    rows = rows_ref[...].astype(f32)
    mean = jnp.mean(rows * rows, axis=1, keepdims=True)
    gain = gain_ref[...].astype(f32).reshape(1, width)
    out_ref[:, :width] = (rows * lax.rsqrt(mean + epsilon) * gain).astype(bf16)
    lane = lax.broadcasted_iota(jnp.int32, (1, 128), 1)
    expert, slot = lane // SLOTS, lane % SLOTS
    count = jnp.zeros((1, 128), jnp.int32)
    token = jnp.full((1, 128), -1.0, f32)
    gate = jnp.zeros((1, 128), f32)
    for t in range(TOK):
        picked = jnp.zeros((1, 128), jnp.int32)
        share = jnp.zeros((1, 128), f32)
        for j in range(8):
            hit = expert == ids_ref[t, j]
            picked = jnp.where(hit, 1, picked)
            share = share + jnp.where(hit, gates_ref[t, j], f32(0.0))
        here = (picked == 1) & (count == slot)
        token = jnp.where(here, f32(t), token)
        gate = jnp.where(here, share, gate)
        count = count + picked
    high = gate.astype(bf16).astype(f32)
    middle = (gate - high).astype(bf16).astype(f32)
    low = gate - high - middle
    row = lax.broadcasted_iota(jnp.int32, (TOK, 128), 0)
    facts = jnp.where(row == 0, token, jnp.where(row == 1, high, jnp.where(row == 2, middle, low)))
    out_ref[:, width:] = facts.astype(bf16)


def prepare(moe_rows, route_ids, route_gates, norm_gain):
    return pl.pallas_call(
        prepare_kernel,
        out_shape=jax.ShapeDtypeStruct((TOK, moe_rows.shape[1] + INFO), bf16),
        in_specs=[SMEM, SMEM, VMEM, VMEM],
        out_specs=VMEM,
        compiler_params=room(4),
    )(route_ids, route_gates, moe_rows, norm_gain)


def grid(rows, columns, dim):
    return lax.broadcasted_iota(jnp.int32, (rows, columns), dim)


def choose_kernel(place_ref, tokens_ref, out_ref):
    ctx, half = place_ref[0], place_ref[2]
    width = out_ref.shape[1]
    first = grid(16, 16, 1) == grid(16, 16, 0) // TOK * TOK
    tokens = jnp.dot(
        first.astype(f32).astype(bf16), tokens_ref[:, width:], preferred_element_type=f32
    )
    row = grid(128, 128, 0)
    lane = half * 32 + row // 8 * SLOTS + row % SLOTS
    pick = (grid(128, 128, 1) == lane).astype(f32).astype(bf16)
    wanted = lax.dot_general(
        pick, tokens.astype(bf16), (((1,), (1,)), ((), ())), preferred_element_type=f32
    )
    row, column = grid(128, 16, 0), grid(128, 16, 1)
    hit = wanted == (column % TOK).astype(f32)
    hit = hit & ((ctx - column // TOK + 4) % 4 == row // SLOTS % 4)
    selector = hit.astype(f32).astype(bf16)
    for low in range(0, width, STEP):
        part = jnp.dot(selector, tokens_ref[:, low : low + STEP], preferred_element_type=f32)
        out_ref[:, low : low + STEP] = part.astype(bf16)


def choose(place, tokens, width):
    return pl.pallas_call(
        choose_kernel,
        out_shape=jax.ShapeDtypeStruct((128, width), bf16),
        in_specs=[SMEM, VMEM],
        out_specs=VMEM,
        compiler_params=room(6),
        cost_estimate=pl.CostEstimate(flops=2 * 128 * 16 * width, bytes_accessed=2 * 144 * width, transcendentals=0),
    )(place, tokens)


def gate_up_kernel(rows_ref, own_ref, other_ref, out_ref, held_ref, sems):
    width = rows_ref.shape[1]
    copies = []
    for i in range(width // STEP):
        part = pl.ds(i * STEP, STEP)
        for j, weight_ref in enumerate((own_ref, other_ref)):
            copies.append(
                pltpu.make_async_copy(weight_ref.at[:, part], held_ref.at[j, :, part], sems.at[i, j])
            )
            copies[-1].start()
    sums = [jnp.zeros((128, 256), f32) for _ in range(4)]
    for i in range(width // STEP):
        low, high = i * STEP, (i + 1) * STEP
        rows = rows_ref[:, low:high]
        for j in range(2):
            copies[2 * i + j].wait()
            for k in range(2):
                sums[2 * j + k] += jnp.dot(rows, held_ref[j, k, low:high], preferred_element_type=f32)
    for j in range(2):
        gate, up = sums[2 * j], sums[2 * j + 1]
        out_ref[:, j * 256 : (j + 1) * 256] = (gate / (1.0 + jnp.exp(-gate)) * up).astype(bf16)


def gate_up(rows, own, other):
    width = rows.shape[1]
    return pl.pallas_call(
        gate_up_kernel,
        out_shape=jax.ShapeDtypeStruct((128, 512), bf16),
        in_specs=[VMEM, HBM, HBM],
        out_specs=VMEM,
        scratch_shapes=[
            pltpu.VMEM((2, 2, width, 256), bf16),
            pltpu.SemaphoreType.DMA((width // STEP, 2)),
        ],
        compiler_params=room(24),
        cost_estimate=pl.CostEstimate(
            flops=2 * 128 * width * 1024, bytes_accessed=2 * width * (1024 + 128), transcendentals=65536
        ),
    )(rows, own, other)


def down_kernel(place_ref, p0, p1, p2, p3, own_ref, other_ref, out_ref, held_ref, sems):
    ctx, core = place_ref[0], place_ref[1]
    copies = []
    for k in range(4):
        source = (ctx - k + 4) % 4
        for j, weight_ref in enumerate((own_ref, other_ref)):
            copies.append(
                pltpu.make_async_copy(weight_ref.at[source], held_ref.at[j, k], sems.at[j, k])
            )
            copies[-1].start()
    totals = [jnp.zeros((128, 896), f32) for _ in range(2)]
    for k, piece in enumerate((p0, p1, p2, p3)):
        for j in range(2):
            copies[2 * k + j].wait()
            totals[j] += jnp.dot(piece[:, :256], held_ref[j, k, core], preferred_element_type=f32)
            totals[j] += jnp.dot(piece[:, 256:], held_ref[j, k, 1 - core], preferred_element_type=f32)
    out_ref[:, :896] = jnp.where(core == 0, totals[0], totals[1]).astype(bf16)
    out_ref[:, 896:] = jnp.where(core == 0, totals[1], totals[0]).astype(bf16)


def down(place, pieces, own, other):
    return pl.pallas_call(
        down_kernel,
        out_shape=jax.ShapeDtypeStruct((128, 1792), bf16),
        in_specs=[SMEM] + [VMEM] * 4 + [HBM] * 2,
        out_specs=VMEM,
        scratch_shapes=[pltpu.VMEM((2, 4, 2, 256, 896), bf16), pltpu.SemaphoreType.DMA((2, 4))],
        compiler_params=room(16),
        cost_estimate=pl.CostEstimate(
            flops=2 * 128 * 2048 * 1792, bytes_accessed=2 * 2048 * 1792 + 2 * 128 * 2048, transcendentals=0
        ),
    )(place, *pieces, own, other)


def mix_kernel(place_ref, back0, back1, facts0, facts1, out_ref):
    ctx, half = place_ref[0], place_ref[2]
    lane = grid(128, 128, 1)
    spread = grid(128, 128, 0) == half * 32 + lane // 8 * SLOTS + lane % SLOTS
    spread = spread.astype(f32).astype(bf16)
    total = jnp.zeros((32, 1792), f32)
    for q, (back, facts) in enumerate(((back0, facts0), (back1, facts1))):
        facts = jnp.dot(facts[...], spread, preferred_element_type=f32)
        at, lane_ctx = grid(16, 128, 0), grid(16, 128, 1) // SLOTS % 4
        here = (ctx - at // TOK + 4) % 4 == lane_ctx
        token, high, middle, low = (
            jnp.sum(jnp.where(here & (at % TOK == i), facts, 0.0), axis=0, keepdims=True) for i in range(4)
        )
        at, lane_ctx = grid(32, 128, 0), grid(32, 128, 1) // SLOTS % 4
        fits = (at // 8 == lane_ctx) & (at // 4 % 2 == (half if q == 0 else 1 - half))
        fits = fits & ((at % TOK).astype(f32) == token)
        for part in (high, middle, low):
            matrix = jnp.where(fits, part, 0.0).astype(bf16)
            total += jnp.dot(matrix, back[...], preferred_element_type=f32)
    out_ref[...] = total.reshape(8, TOK, 1792).astype(bf16)


def mix(place, back0, back1, facts0, facts1):
    return pl.pallas_call(
        mix_kernel,
        out_shape=jax.ShapeDtypeStruct((8, TOK, 1792), bf16),
        in_specs=[SMEM] + [VMEM] * 4,
        out_specs=VMEM,
        compiler_params=room(6),
        cost_estimate=pl.CostEstimate(flops=2 * 32 * 256 * 1792 * 3, bytes_accessed=1 << 20, transcendentals=0),
    )(place, back0, back1, facts0, facts1)


def shards(
    query_latent,
    query_rope,
    latent_cache,
    rope_keys,
    lengths,
    moe_rows,
    route_ids,
    route_gates,
    norm_gain,
    expert_in,
    expert_out,
):
    c = lax.axis_index("ctx")
    a = lax.axis_index("att")
    h = lax.axis_index("zhi")
    width = moe_rows.shape[1]
    swap_core = [(0, 1), (1, 0)]

    place = jnp.stack([c, a, h]).astype(jnp.int32)
    payload = prepare(moe_rows, route_ids, route_gates, norm_gain)

    def hop(value, k, flip):
        pairs = [
            (i * 2 + j, (i + k) % 4 * 2 + (j ^ flip)) for i in range(4) for j in range(2)
        ]
        return lax.ppermute(value, ("ctx", "zhi"), pairs)

    def rows_of(half):
        tokens = jnp.concatenate(half, axis=0)
        return choose(place, tokens, width), tokens[:, width:]

    def across(value):
        value = value.reshape(16, 8, value.shape[1])
        moved = lax.all_to_all(value, ("x", "y"), split_axis=0, concat_axis=0, tiled=True)
        return moved.reshape(128, moved.shape[2])

    def hidden_of(got):
        hidden = gate_up(got, weight_in, other_in)
        return [hidden] + [hop(hidden, k, 0) for k in (1, 2, 3)]

    rows0, facts0 = rows_of([payload] + [hop(payload, k, 0) for k in (1, 2, 3)])
    weight_in, weight_out = expert_in[0], expert_out[0].reshape(4, 2, 256, 896)
    rows0, facts0, payload, moving_in, moving_out = lax.optimization_barrier(
        (rows0, facts0, payload, weight_in, weight_out)
    )
    got0 = across(rows0)
    other_in = lax.ppermute(moving_in, "att", swap_core)
    other_out = lax.ppermute(moving_out, "att", swap_core)
    rows1, facts1 = rows_of([hop(payload, k, 1) for k in (0, 1, 2, 3)])
    part = attend(query_latent, query_rope, latent_cache, rope_keys, lengths)
    rows1, facts1, got0, part = lax.optimization_barrier((rows1, facts1, got0, part))
    got1 = across(rows1)

    pieces0 = hidden_of(got0)
    part = part.reshape(4, 32, 640)
    summed = lax.dynamic_index_in_dim(part, c, 0, keepdims=False)
    for k in (1, 2, 3):
        sent = lax.dynamic_index_in_dim(part, (c + k) % 4, 0, keepdims=False)
        summed = summed + lax.ppermute(sent, "ctx", [(i, (i + k) % 4) for i in range(4)])
    attended = finish_attention(summed)
    result0 = down(place, pieces0, weight_out, other_out)
    got1, result0, attended = lax.optimization_barrier((got1, result0, attended))
    back0 = across(result0)
    pieces1 = hidden_of(got1)
    pieces1[0], back0 = lax.optimization_barrier((pieces1[0], back0))
    result1 = down(place, pieces1, weight_out, other_out)
    back1 = across(result1)

    outgoing = mix(place, back0, back1, facts0, facts1)
    final = lax.all_to_all(outgoing, ("ctx", "zhi"), split_axis=0, concat_axis=0, tiled=True)
    final = final.reshape(4, 2, TOK, 1792).astype(f32)
    routed = (final[:, 0] + final[:, 1]).transpose(1, 0, 2).reshape(TOK, 4 * 1792)
    return (attended, routed.astype(bf16))


def solution(mesh):
    fine = Mesh(mesh.devices.reshape(4, 2, 2, 4, 4), ("ctx", "att", "zhi", "x", "y"))
    exp = ("zhi", "x", "y")
    sequences = ("att",) + exp
    every = ("ctx", "att") + exp
    placed = (
        P(sequences, None, None),
        P(sequences, None, None),
        P(sequences, "ctx", None),
        P(sequences, None, "ctx"),
        P(sequences),
        P(every, None),
        P(every, None),
        P(every, None),
        P(),
        P(exp, None, None, ("ctx", "att")),
        P(exp, None, ("ctx", "att")),
    )
    return jax.shard_map(
        shards,
        mesh=fine,
        in_specs=placed,
        out_specs=(P(sequences, "ctx", None), P(every, None)),
        check_vma=False,
    )
```

```python
import jax
import jax.numpy as jnp
from jax import lax
from jax.experimental import pallas as pl
from jax.experimental.pallas import tpu as pltpu
from jax.sharding import Mesh, PartitionSpec as P

softmax_scale = 192.0 ** (-0.5)
epsilon = 1e-06
bf16 = jnp.bfloat16
f32 = jnp.float32
INFO = 128
TOK = 4
SLOTS = 2


def attend(query_latent, query_rope, latent_cache, rope_keys, lengths):
    shard_length = latent_cache.shape[1]
    first_position = lax.axis_index("ctx") * shard_length
    scores = jnp.einsum("hr,tr->ht", query_latent[0], latent_cache[0], preferred_element_type=f32)
    scores = scores + jnp.einsum("hp,pt->ht", query_rope[0], rope_keys[0], preferred_element_type=f32)
    position = first_position + jnp.arange(shard_length, dtype=jnp.int32)
    live_mask = position < lengths[0]
    weights = jnp.where(live_mask[None, :], jnp.exp(softmax_scale * scores), f32(0.0))
    mass = jnp.sum(weights, axis=1, keepdims=True)
    numerator = jnp.dot(weights.astype(bf16), latent_cache[0], preferred_element_type=f32)
    high = lax.reduce_precision(mass, 8, 7)
    low = mass - high
    tail = jnp.concatenate([jnp.broadcast_to(v, (128, 64)) for v in (high, low)], axis=1)
    return jnp.concatenate([numerator, tail], axis=1).astype(bf16)


def finish_attention(parts):
    summed = sum(v.astype(f32) for v in parts)
    return (summed[:, :512] / (summed[:, 512:513] + summed[:, 576:577])).astype(bf16)[None]


VMEM = pl.BlockSpec(memory_space=pltpu.VMEM)
SMEM = pl.BlockSpec(memory_space=pltpu.SMEM)
HBM = pl.BlockSpec(memory_space=pltpu.HBM)
STEP = 1024


def room(mib):
    return pltpu.CompilerParams(vmem_limit_bytes=mib * 1024 * 1024)


def prepare_kernel(ids_ref, gates_ref, rows_ref, gain_ref, out_ref):
    width = rows_ref.shape[1]
    rows = rows_ref[...].astype(f32)
    mean = jnp.mean(rows * rows, axis=1, keepdims=True)
    gain = gain_ref[...].astype(f32).reshape(1, width)
    out_ref[:, :width] = (rows * lax.rsqrt(mean + epsilon) * gain).astype(bf16)
    lane = lax.broadcasted_iota(jnp.int32, (1, 128), 1)
    expert, slot = lane // SLOTS, lane % SLOTS
    count = jnp.zeros((1, 128), jnp.int32)
    token = jnp.full((1, 128), -1.0, f32)
    gate = jnp.zeros((1, 128), f32)
    for t in range(TOK):
        picked = jnp.zeros((1, 128), jnp.int32)
        share = jnp.zeros((1, 128), f32)
        for j in range(8):
            hit = expert == ids_ref[t, j]
            picked = jnp.where(hit, 1, picked)
            share = share + jnp.where(hit, gates_ref[t, j], f32(0.0))
        here = (picked == 1) & (count == slot)
        token = jnp.where(here, f32(t), token)
        gate = jnp.where(here, share, gate)
        count = count + picked
    high = gate.astype(bf16).astype(f32)
    middle = (gate - high).astype(bf16).astype(f32)
    low = gate - high - middle
    row = lax.broadcasted_iota(jnp.int32, (TOK, 128), 0)
    facts = jnp.where(row == 0, token, jnp.where(row == 1, high, jnp.where(row == 2, middle, low)))
    out_ref[:, width:] = facts.astype(bf16)


def prepare(moe_rows, route_ids, route_gates, norm_gain):
    return pl.pallas_call(
        prepare_kernel,
        out_shape=jax.ShapeDtypeStruct((TOK, moe_rows.shape[1] + INFO), bf16),
        in_specs=[SMEM, SMEM, VMEM, VMEM],
        out_specs=VMEM,
    )(route_ids, route_gates, moe_rows, norm_gain)


def grid(rows, columns, dim):
    return lax.broadcasted_iota(jnp.int32, (rows, columns), dim)


def choose_kernel(place_ref, tokens_ref, out_ref):
    ctx, half = place_ref[0], place_ref[2]
    width = out_ref.shape[1]
    first = grid(16, 16, 1) == grid(16, 16, 0) // TOK * TOK
    tokens = jnp.dot(
        first.astype(f32).astype(bf16), tokens_ref[:, width:], preferred_element_type=f32
    )
    row = grid(128, 128, 0)
    lane = half * 32 + row // 8 * SLOTS + row % SLOTS
    pick = (grid(128, 128, 1) == lane).astype(f32).astype(bf16)
    wanted = lax.dot_general(
        pick, tokens.astype(bf16), (((1,), (1,)), ((), ())), preferred_element_type=f32
    )
    row, column = grid(128, 16, 0), grid(128, 16, 1)
    hit = wanted == (column % TOK).astype(f32)
    hit = hit & ((ctx - column // TOK + 4) % 4 == row // SLOTS % 4)
    selector = hit.astype(f32).astype(bf16)
    for low in range(0, width, STEP):
        part = jnp.dot(selector, tokens_ref[:, low : low + STEP], preferred_element_type=f32)
        out_ref[:, low : low + STEP] = part.astype(bf16)


def choose(place, tokens, width):
    return pl.pallas_call(
        choose_kernel,
        out_shape=jax.ShapeDtypeStruct((128, width), bf16),
        in_specs=[SMEM, VMEM],
        out_specs=VMEM,
        compiler_params=room(6),
        cost_estimate=pl.CostEstimate(flops=2 * 128 * 16 * width, bytes_accessed=2 * 144 * width, transcendentals=0),
    )(place, tokens)


def gate_up_kernel(rows_ref, own_ref, other_ref, out_ref, held_ref, sems):
    width = rows_ref.shape[1]
    copies = []
    for i in range(width // STEP):
        part = pl.ds(i * STEP, STEP)
        for j, weight_ref in enumerate((own_ref, other_ref)):
            copies.append(
                pltpu.make_async_copy(weight_ref.at[:, part], held_ref.at[j, :, part], sems.at[i, j])
            )
            copies[-1].start()
    sums = [jnp.zeros((128, 256), f32) for _ in range(4)]
    for i in range(width // STEP):
        low, high = i * STEP, (i + 1) * STEP
        rows = rows_ref[:, low:high]
        for j in range(2):
            copies[2 * i + j].wait()
            for k in range(2):
                sums[2 * j + k] += jnp.dot(rows, held_ref[j, k, low:high], preferred_element_type=f32)
    for j in range(2):
        gate, up = sums[2 * j], sums[2 * j + 1]
        out_ref[:, j * 256 : (j + 1) * 256] = (gate / (1.0 + jnp.exp(-gate)) * up).astype(bf16)


def gate_up(rows, own, other):
    width = rows.shape[1]
    return pl.pallas_call(
        gate_up_kernel,
        out_shape=jax.ShapeDtypeStruct((128, 512), bf16),
        in_specs=[VMEM, HBM, HBM],
        out_specs=VMEM,
        scratch_shapes=[
            pltpu.VMEM((2, 2, width, 256), bf16),
            pltpu.SemaphoreType.DMA((width // STEP, 2)),
        ],
        compiler_params=room(57),
        cost_estimate=pl.CostEstimate(
            flops=2 * 128 * width * 1024, bytes_accessed=2 * width * (1024 + 128), transcendentals=65536
        ),
    )(rows, own, other)


def down_kernel(place_ref, p0, p1, p2, p3, own_ref, other_ref, out_ref, held_ref, sems):
    ctx, core = place_ref[0], place_ref[1]
    copies = []
    for k in range(4):
        source = (ctx - k + 4) % 4
        for j, weight_ref in enumerate((own_ref, other_ref)):
            copies.append(
                pltpu.make_async_copy(weight_ref.at[source], held_ref.at[j, k], sems.at[j, k])
            )
            copies[-1].start()
    totals = [jnp.zeros((128, 896), f32) for _ in range(2)]
    for k, piece in enumerate((p0, p1, p2, p3)):
        for j in range(2):
            copies[2 * k + j].wait()
            totals[j] += jnp.dot(piece[:, :256], held_ref[j, k, core], preferred_element_type=f32)
            totals[j] += jnp.dot(piece[:, 256:], held_ref[j, k, 1 - core], preferred_element_type=f32)
    out_ref[:, :896] = jnp.where(core == 0, totals[0], totals[1]).astype(bf16)
    out_ref[:, 896:] = jnp.where(core == 0, totals[1], totals[0]).astype(bf16)


def down(place, pieces, own, other):
    return pl.pallas_call(
        down_kernel,
        out_shape=jax.ShapeDtypeStruct((128, 1792), bf16),
        in_specs=[SMEM] + [VMEM] * 4 + [HBM] * 2,
        out_specs=VMEM,
        scratch_shapes=[pltpu.VMEM((2, 4, 2, 256, 896), bf16), pltpu.SemaphoreType.DMA((2, 4))],
        compiler_params=room(58),
        cost_estimate=pl.CostEstimate(
            flops=2 * 128 * 2048 * 1792, bytes_accessed=2 * 2048 * 1792 + 2 * 128 * 2048, transcendentals=0
        ),
    )(place, *pieces, own, other)


def mix_kernel(place_ref, back0, back1, facts0, facts1, out_ref):
    ctx, half = place_ref[0], place_ref[2]
    lane = grid(128, 128, 1)
    spread = grid(128, 128, 0) == half * 32 + lane // 8 * SLOTS + lane % SLOTS
    spread = spread.astype(f32).astype(bf16)
    total = jnp.zeros((32, 1792), f32)
    for q, (back, facts) in enumerate(((back0, facts0), (back1, facts1))):
        facts = jnp.dot(facts[...], spread, preferred_element_type=f32)
        at, lane_ctx = grid(16, 128, 0), grid(16, 128, 1) // SLOTS % 4
        here = (ctx - at // TOK + 4) % 4 == lane_ctx
        token, high, middle, low = (
            jnp.sum(jnp.where(here & (at % TOK == i), facts, 0.0), axis=0, keepdims=True) for i in range(4)
        )
        at, lane_ctx = grid(32, 128, 0), grid(32, 128, 1) // SLOTS % 4
        fits = (at // 8 == lane_ctx) & (at // 4 % 2 == (half if q == 0 else 1 - half))
        fits = fits & ((at % TOK).astype(f32) == token)
        for part in (high, middle, low):
            matrix = jnp.where(fits, part, 0.0).astype(bf16)
            total += jnp.dot(matrix, back[...], preferred_element_type=f32)
    out_ref[...] = total.reshape(8, TOK, 1792).astype(bf16)


def mix(place, back0, back1, facts0, facts1):
    return pl.pallas_call(
        mix_kernel,
        out_shape=jax.ShapeDtypeStruct((8, TOK, 1792), bf16),
        in_specs=[SMEM] + [VMEM] * 4,
        out_specs=VMEM,
        compiler_params=room(6),
        cost_estimate=pl.CostEstimate(flops=2 * 32 * 256 * 1792 * 3, bytes_accessed=1 << 20, transcendentals=0),
    )(place, back0, back1, facts0, facts1)


def shards(
    query_latent,
    query_rope,
    latent_cache,
    rope_keys,
    lengths,
    moe_rows,
    route_ids,
    route_gates,
    norm_gain,
    expert_in,
    expert_out,
):
    c = lax.axis_index("ctx")
    a = lax.axis_index("att")
    h = lax.axis_index("zhi")
    width = moe_rows.shape[1]
    swap_core = [(0, 1), (1, 0)]

    place = jnp.stack([c, a, h]).astype(jnp.int32)
    payload = prepare(moe_rows, route_ids, route_gates, norm_gain)

    def hop(value, k, flip):
        pairs = [
            (i * 2 + j, (i + k) % 4 * 2 + (j ^ flip)) for i in range(4) for j in range(2)
        ]
        return lax.ppermute(value, ("ctx", "zhi"), pairs)

    def rows_of(half):
        tokens = jnp.concatenate(half, axis=0)
        return choose(place, tokens, width), tokens[:, width:]

    def across(value):
        value = value.reshape(16, 8, value.shape[1])
        moved = lax.all_to_all(value, ("x", "y"), split_axis=0, concat_axis=0, tiled=True)
        return moved.reshape(128, moved.shape[2])

    def hidden_of(got):
        hidden = gate_up(got, weight_in, other_in)
        return [hidden] + [hop(hidden, k, 0) for k in (1, 2, 3)]

    rows0, facts0 = rows_of([payload] + [hop(payload, k, 0) for k in (1, 2, 3)])
    weight_in, weight_out = expert_in[0], expert_out[0].reshape(4, 2, 256, 896)
    rows0, facts0, payload, moving_in, moving_out = lax.optimization_barrier(
        (rows0, facts0, payload, weight_in, weight_out)
    )
    got0 = across(rows0)
    other_in = lax.ppermute(moving_in, "att", swap_core)
    other_out = lax.ppermute(moving_out, "att", swap_core)
    rows1, facts1 = rows_of([hop(payload, k, 1) for k in (0, 1, 2, 3)])
    part = attend(query_latent, query_rope, latent_cache, rope_keys, lengths)
    rows1, facts1, got0, part = lax.optimization_barrier((rows1, facts1, got0, part))
    got1 = across(rows1)

    pieces0 = hidden_of(got0)
    pieces0[0], part = lax.optimization_barrier((pieces0[0], part))
    part = part.reshape(4, 32, 640)
    parts = [lax.dynamic_index_in_dim(part, c, 0, keepdims=False)]
    for k in (1, 2, 3):
        sent = lax.dynamic_index_in_dim(part, (c + k) % 4, 0, keepdims=False)
        parts.append(lax.ppermute(sent, "ctx", [(i, (i + k) % 4) for i in range(4)]))
    attended = finish_attention(parts)
    result0 = down(place, pieces0, weight_out, other_out)
    back0 = across(result0)
    got1, attended, _ = lax.optimization_barrier((got1, attended, result0))
    pieces1 = hidden_of(got1)
    pieces1[0], back0 = lax.optimization_barrier((pieces1[0], back0))
    result1 = down(place, pieces1, weight_out, other_out)
    back1 = across(result1)

    outgoing = mix(place, back0, back1, facts0, facts1)
    final = lax.all_to_all(outgoing, ("ctx", "zhi"), split_axis=0, concat_axis=0, tiled=True)
    final = final.reshape(4, 2, TOK, 1792).astype(f32)
    routed = (final[:, 0] + final[:, 1]).transpose(1, 0, 2).reshape(TOK, 4 * 1792)
    return (attended, routed.astype(bf16))


def solution(mesh):
    fine = Mesh(mesh.devices.reshape(4, 2, 2, 4, 4), ("ctx", "att", "zhi", "x", "y"))
    exp = ("zhi", "x", "y")
    sequences = ("att",) + exp
    every = ("ctx", "att") + exp
    placed = (
        P(sequences, None, None),
        P(sequences, None, None),
        P(sequences, "ctx", None),
        P(sequences, None, "ctx"),
        P(sequences),
        P(every, None),
        P(every, None),
        P(every, None),
        P(),
        P(exp, None, None, ("ctx", "att")),
        P(exp, None, ("ctx", "att")),
    )
    return jax.shard_map(
        shards,
        mesh=fine,
        in_specs=placed,
        out_specs=(P(sequences, "ctx", None), P(every, None)),
        check_vma=False,
    )
```

```python
import jax
import jax.numpy as jnp
from jax import lax
from jax.experimental import pallas as pl
from jax.experimental.pallas import tpu as pltpu
from jax.sharding import Mesh, PartitionSpec as P

softmax_scale = 192.0 ** (-0.5)
epsilon = 1e-06
bf16 = jnp.bfloat16
f32 = jnp.float32
INFO = 128
TOK = 4
SLOTS = 2


def attend(query_latent, query_rope, latent_cache, rope_keys, lengths):
    shard_length = latent_cache.shape[1]
    first_position = lax.axis_index("ctx") * shard_length
    scores = jnp.einsum("hr,tr->ht", query_latent[0], latent_cache[0], preferred_element_type=f32)
    scores = scores + jnp.einsum("hp,pt->ht", query_rope[0], rope_keys[0], preferred_element_type=f32)
    position = first_position + jnp.arange(shard_length, dtype=jnp.int32)
    live_mask = position < lengths[0]
    weights = jnp.where(live_mask[None, :], jnp.exp(softmax_scale * scores), f32(0.0))
    mass = jnp.sum(weights, axis=1, keepdims=True)
    numerator = jnp.dot(weights.astype(bf16), latent_cache[0], preferred_element_type=f32)
    high = lax.reduce_precision(mass, 8, 7)
    low = mass - high
    tail = jnp.concatenate([jnp.broadcast_to(v, (128, 64)) for v in (high, low)], axis=1)
    return jnp.concatenate([numerator, tail], axis=1).astype(bf16)


def finish_attention(parts):
    summed = sum(v.astype(f32) for v in parts)
    return (summed[:, :512] / (summed[:, 512:513] + summed[:, 576:577])).astype(bf16)[None]


VMEM = pl.BlockSpec(memory_space=pltpu.VMEM)
SMEM = pl.BlockSpec(memory_space=pltpu.SMEM)
HBM = pl.BlockSpec(memory_space=pltpu.HBM)
STEP = 1024


def room(mib):
    return pltpu.CompilerParams(vmem_limit_bytes=mib * 1024 * 1024)


def prepare_kernel(ids_ref, gates_ref, rows_ref, gain_ref, out_ref):
    width = rows_ref.shape[1]
    rows = rows_ref[...].astype(f32)
    mean = jnp.mean(rows * rows, axis=1, keepdims=True)
    gain = gain_ref[...].astype(f32).reshape(1, width)
    out_ref[:, :width] = (rows * lax.rsqrt(mean + epsilon) * gain).astype(bf16)
    lane = lax.broadcasted_iota(jnp.int32, (1, 128), 1)
    expert, slot = lane // SLOTS, lane % SLOTS
    count = jnp.zeros((1, 128), jnp.int32)
    token = jnp.full((1, 128), -1.0, f32)
    gate = jnp.zeros((1, 128), f32)
    for t in range(TOK):
        picked = jnp.zeros((1, 128), jnp.int32)
        share = jnp.zeros((1, 128), f32)
        for j in range(8):
            hit = expert == ids_ref[t, j]
            picked = jnp.where(hit, 1, picked)
            share = share + jnp.where(hit, gates_ref[t, j], f32(0.0))
        here = (picked == 1) & (count == slot)
        token = jnp.where(here, f32(t), token)
        gate = jnp.where(here, share, gate)
        count = count + picked
    high = gate.astype(bf16).astype(f32)
    middle = (gate - high).astype(bf16).astype(f32)
    low = gate - high - middle
    row = lax.broadcasted_iota(jnp.int32, (TOK, 128), 0)
    facts = jnp.where(row == 0, token, jnp.where(row == 1, high, jnp.where(row == 2, middle, low)))
    out_ref[:, width:] = facts.astype(bf16)


def prepare(moe_rows, route_ids, route_gates, norm_gain):
    return pl.pallas_call(
        prepare_kernel,
        out_shape=jax.ShapeDtypeStruct((TOK, moe_rows.shape[1] + INFO), bf16),
        in_specs=[SMEM, SMEM, VMEM, VMEM],
        out_specs=VMEM,
    )(route_ids, route_gates, moe_rows, norm_gain)


def grid(rows, columns, dim):
    return lax.broadcasted_iota(jnp.int32, (rows, columns), dim)


def choose_kernel(place_ref, tokens_ref, out_ref):
    ctx, half = place_ref[0], place_ref[2]
    width = out_ref.shape[1]
    first = grid(16, 16, 1) == grid(16, 16, 0) // TOK * TOK
    tokens = jnp.dot(
        first.astype(f32).astype(bf16), tokens_ref[:, width:], preferred_element_type=f32
    )
    row = grid(128, 128, 0)
    lane = half * 32 + row // 8 * SLOTS + row % SLOTS
    pick = (grid(128, 128, 1) == lane).astype(f32).astype(bf16)
    wanted = lax.dot_general(
        pick, tokens.astype(bf16), (((1,), (1,)), ((), ())), preferred_element_type=f32
    )
    row, column = grid(128, 16, 0), grid(128, 16, 1)
    hit = wanted == (column % TOK).astype(f32)
    hit = hit & ((ctx - column // TOK + 4) % 4 == row // SLOTS % 4)
    selector = hit.astype(f32).astype(bf16)
    for low in range(0, width, STEP):
        part = jnp.dot(selector, tokens_ref[:, low : low + STEP], preferred_element_type=f32)
        out_ref[:, low : low + STEP] = part.astype(bf16)


def choose(place, tokens, width):
    return pl.pallas_call(
        choose_kernel,
        out_shape=jax.ShapeDtypeStruct((128, width), bf16),
        in_specs=[SMEM, VMEM],
        out_specs=VMEM,
        compiler_params=room(6),
        cost_estimate=pl.CostEstimate(flops=2 * 128 * 16 * width, bytes_accessed=2 * 144 * width, transcendentals=0),
    )(place, tokens)


def gate_up_kernel(rows_hbm, own_hbm, other_hbm, out_ref, rows_ref, held_ref, sems):
    width = rows_ref.shape[1]
    copies = []
    for i in range(width // STEP):
        part = pl.ds(i * STEP, STEP)
        copies.append(
            [
                pltpu.make_async_copy(rows_hbm.at[:, part], rows_ref.at[:, part], sems.at[i, 0]),
                pltpu.make_async_copy(own_hbm.at[:, part], held_ref.at[0, :, part], sems.at[i, 1]),
                pltpu.make_async_copy(other_hbm.at[:, part], held_ref.at[1, :, part], sems.at[i, 2]),
            ]
        )
        for copy in copies[-1]:
            copy.start()
    sums = [jnp.zeros((128, 256), f32) for _ in range(4)]
    for i in range(width // STEP):
        low, high = i * STEP, (i + 1) * STEP
        for copy in copies[i]:
            copy.wait()
        rows = rows_ref[:, low:high]
        for j in range(2):
            for k in range(2):
                sums[2 * j + k] += jnp.dot(rows, held_ref[j, k, low:high], preferred_element_type=f32)
    for j in range(2):
        gate, up = sums[2 * j], sums[2 * j + 1]
        out_ref[:, j * 256 : (j + 1) * 256] = (gate / (1.0 + jnp.exp(-gate)) * up).astype(bf16)


def gate_up(rows, own, other):
    width = rows.shape[1]
    return pl.pallas_call(
        gate_up_kernel,
        out_shape=jax.ShapeDtypeStruct((128, 512), bf16),
        in_specs=[HBM] * 3,
        out_specs=VMEM,
        scratch_shapes=[
            pltpu.VMEM((128, width), bf16),
            pltpu.VMEM((2, 2, width, 256), bf16),
            pltpu.SemaphoreType.DMA((width // STEP, 3)),
        ],
        compiler_params=room(55),
        cost_estimate=pl.CostEstimate(
            flops=2 * 128 * width * 1024, bytes_accessed=2 * width * (1024 + 128), transcendentals=65536
        ),
    )(rows, own, other)


def down_kernel(place_ref, p0, p1, p2, p3, own_hbm, other_hbm, out_ref, pieces_ref, held_ref, sems):
    ctx, core = place_ref[0], place_ref[1]
    copies = []
    for k, piece in enumerate((p0, p1, p2, p3)):
        source = (ctx - k + 4) % 4
        copies.append(
            [
                pltpu.make_async_copy(piece, pieces_ref.at[k], sems.at[k, 0]),
                pltpu.make_async_copy(own_hbm.at[source], held_ref.at[0, k], sems.at[k, 1]),
                pltpu.make_async_copy(other_hbm.at[source], held_ref.at[1, k], sems.at[k, 2]),
            ]
        )
        for copy in copies[-1]:
            copy.start()
    totals = [jnp.zeros((128, 896), f32) for _ in range(2)]
    for k in range(4):
        for copy in copies[k]:
            copy.wait()
        for j in range(2):
            totals[j] += jnp.dot(pieces_ref[k, :, :256], held_ref[j, k, core], preferred_element_type=f32)
            totals[j] += jnp.dot(pieces_ref[k, :, 256:], held_ref[j, k, 1 - core], preferred_element_type=f32)
    out_ref[:, :896] = jnp.where(core == 0, totals[0], totals[1]).astype(bf16)
    out_ref[:, 896:] = jnp.where(core == 0, totals[1], totals[0]).astype(bf16)


def down(place, pieces, own, other):
    return pl.pallas_call(
        down_kernel,
        out_shape=jax.ShapeDtypeStruct((128, 1792), bf16),
        in_specs=[SMEM] + [HBM] * 6,
        out_specs=VMEM,
        scratch_shapes=[
            pltpu.VMEM((4, 128, 512), bf16),
            pltpu.VMEM((2, 4, 2, 256, 896), bf16),
            pltpu.SemaphoreType.DMA((4, 3)),
        ],
        compiler_params=room(57),
        cost_estimate=pl.CostEstimate(
            flops=2 * 128 * 2048 * 1792, bytes_accessed=2 * 2048 * 1792 + 2 * 128 * 2048, transcendentals=0
        ),
    )(place, *pieces, own, other)


def mix_kernel(place_ref, back0, back1, facts0, facts1, out_ref):
    ctx, half = place_ref[0], place_ref[2]
    lane = grid(128, 128, 1)
    spread = grid(128, 128, 0) == half * 32 + lane // 8 * SLOTS + lane % SLOTS
    spread = spread.astype(f32).astype(bf16)
    total = jnp.zeros((32, 1792), f32)
    for q, (back, facts) in enumerate(((back0, facts0), (back1, facts1))):
        facts = jnp.dot(facts[...], spread, preferred_element_type=f32)
        at, lane_ctx = grid(16, 128, 0), grid(16, 128, 1) // SLOTS % 4
        here = (ctx - at // TOK + 4) % 4 == lane_ctx
        token, high, middle, low = (
            jnp.sum(jnp.where(here & (at % TOK == i), facts, 0.0), axis=0, keepdims=True) for i in range(4)
        )
        at, lane_ctx = grid(32, 128, 0), grid(32, 128, 1) // SLOTS % 4
        fits = (at // 8 == lane_ctx) & (at // 4 % 2 == (half if q == 0 else 1 - half))
        fits = fits & ((at % TOK).astype(f32) == token)
        for part in (high, middle, low):
            matrix = jnp.where(fits, part, 0.0).astype(bf16)
            total += jnp.dot(matrix, back[...], preferred_element_type=f32)
    out_ref[...] = total.reshape(8, TOK, 1792).astype(bf16)


def mix(place, back0, back1, facts0, facts1):
    return pl.pallas_call(
        mix_kernel,
        out_shape=jax.ShapeDtypeStruct((8, TOK, 1792), bf16),
        in_specs=[SMEM] + [VMEM] * 4,
        out_specs=VMEM,
        compiler_params=room(6),
        cost_estimate=pl.CostEstimate(flops=2 * 32 * 256 * 1792 * 3, bytes_accessed=1 << 20, transcendentals=0),
    )(place, back0, back1, facts0, facts1)


def shards(
    query_latent,
    query_rope,
    latent_cache,
    rope_keys,
    lengths,
    moe_rows,
    route_ids,
    route_gates,
    norm_gain,
    expert_in,
    expert_out,
):
    c = lax.axis_index("ctx")
    a = lax.axis_index("att")
    h = lax.axis_index("zhi")
    width = moe_rows.shape[1]
    swap_core = [(0, 1), (1, 0)]

    place = jnp.stack([c, a, h]).astype(jnp.int32)
    payload = prepare(moe_rows, route_ids, route_gates, norm_gain)

    def hop(value, k, flip):
        pairs = [
            (i * 2 + j, (i + k) % 4 * 2 + (j ^ flip)) for i in range(4) for j in range(2)
        ]
        return lax.ppermute(value, ("ctx", "zhi"), pairs)

    def rows_of(half):
        tokens = jnp.concatenate(half, axis=0)
        return choose(place, tokens, width), tokens[:, width:]

    def across(value):
        value = value.reshape(16, 8, value.shape[1])
        moved = lax.all_to_all(value, ("x", "y"), split_axis=0, concat_axis=0, tiled=True)
        return moved.reshape(128, moved.shape[2])

    def hidden_of(got):
        hidden = gate_up(got, weight_in, other_in)
        return [hidden] + [hop(hidden, k, 0) for k in (1, 2, 3)]

    rows0, facts0 = rows_of([payload] + [hop(payload, k, 0) for k in (1, 2, 3)])
    weight_in, weight_out = expert_in[0], expert_out[0].reshape(4, 2, 256, 896)
    rows0, facts0, payload, moving_in, moving_out = lax.optimization_barrier(
        (rows0, facts0, payload, weight_in, weight_out)
    )
    got0 = across(rows0)
    other_in = lax.ppermute(moving_in, "att", swap_core)
    other_out = lax.ppermute(moving_out, "att", swap_core)
    rows1, facts1 = rows_of([hop(payload, k, 1) for k in (0, 1, 2, 3)])
    rows1, facts1, got0 = lax.optimization_barrier((rows1, facts1, got0))
    got1 = across(rows1)

    pieces0 = hidden_of(got0)
    query_latent, query_rope, pieces0[0] = lax.optimization_barrier((query_latent, query_rope, pieces0[0]))
    part = attend(query_latent, query_rope, latent_cache, rope_keys, lengths).reshape(4, 32, 640)
    result0 = down(place, pieces0, weight_out, other_out)
    back0 = across(result0)
    got1, part, _ = lax.optimization_barrier((got1, part, result0))
    pieces1 = hidden_of(got1)
    pieces1[2], back0 = lax.optimization_barrier((pieces1[2], back0))
    result1 = down(place, pieces1, weight_out, other_out)
    back1 = across(result1)
    part, _ = lax.optimization_barrier((part, result1))
    parts = [lax.dynamic_index_in_dim(part, c, 0, keepdims=False)]
    for k in (1, 2, 3):
        sent = lax.dynamic_index_in_dim(part, (c + k) % 4, 0, keepdims=False)
        parts.append(lax.ppermute(sent, "ctx", [(i, (i + k) % 4) for i in range(4)]))
    attended = finish_attention(parts)

    outgoing = mix(place, back0, back1, facts0, facts1)
    final = lax.all_to_all(outgoing, ("ctx", "zhi"), split_axis=0, concat_axis=0, tiled=True)
    final = final.reshape(4, 2, TOK, 1792).astype(f32)
    routed = (final[:, 0] + final[:, 1]).transpose(1, 0, 2).reshape(TOK, 4 * 1792)
    return (attended, routed.astype(bf16))


def solution(mesh):
    fine = Mesh(mesh.devices.reshape(4, 2, 2, 4, 4), ("ctx", "att", "zhi", "x", "y"))
    exp = ("zhi", "x", "y")
    sequences = ("att",) + exp
    every = ("ctx", "att") + exp
    placed = (
        P(sequences, None, None),
        P(sequences, None, None),
        P(sequences, "ctx", None),
        P(sequences, None, "ctx"),
        P(sequences),
        P(every, None),
        P(every, None),
        P(every, None),
        P(),
        P(exp, None, None, ("ctx", "att")),
        P(exp, None, ("ctx", "att")),
    )
    return jax.shard_map(
        shards,
        mesh=fine,
        in_specs=placed,
        out_specs=(P(sequences, "ctx", None), P(every, None)),
        check_vma=False,
    )
```

```python
import jax
import jax.numpy as jnp
from jax import lax
from jax.experimental import pallas as pl
from jax.experimental.pallas import tpu as pltpu
from jax.sharding import Mesh, PartitionSpec as P

softmax_scale = 192.0 ** (-0.5)
epsilon = 1e-06
bf16 = jnp.bfloat16
f32 = jnp.float32
INFO = 128
TOK = 4
SLOTS = 2


def attend(query_latent, query_rope, latent_cache, rope_keys, lengths):
    shard_length = latent_cache.shape[1]
    first_position = lax.axis_index("ctx") * shard_length
    scores = jnp.einsum("hr,tr->ht", query_latent[0], latent_cache[0], preferred_element_type=f32)
    scores = scores + jnp.einsum("hp,pt->ht", query_rope[0], rope_keys[0], preferred_element_type=f32)
    position = first_position + jnp.arange(shard_length, dtype=jnp.int32)
    live_mask = position < lengths[0]
    weights = jnp.where(live_mask[None, :], jnp.exp(softmax_scale * scores), f32(0.0))
    mass = jnp.sum(weights, axis=1, keepdims=True)
    numerator = jnp.dot(weights.astype(bf16), latent_cache[0], preferred_element_type=f32)
    high = lax.reduce_precision(mass, 8, 7)
    low = mass - high
    tail = jnp.concatenate([jnp.broadcast_to(v, (128, 64)) for v in (high, low)], axis=1)
    return jnp.concatenate([numerator, tail], axis=1).astype(bf16)


def finish_attention(parts):
    summed = sum(v.astype(f32) for v in parts)
    return (summed[:, :512] / (summed[:, 512:513] + summed[:, 576:577])).astype(bf16)[None]


VMEM = pl.BlockSpec(memory_space=pltpu.VMEM)
SMEM = pl.BlockSpec(memory_space=pltpu.SMEM)
HBM = pl.BlockSpec(memory_space=pltpu.HBM)
ANY = pl.BlockSpec(memory_space=pl.ANY)
STEP = 1024


def room(mib):
    return pltpu.CompilerParams(vmem_limit_bytes=mib * 1024 * 1024)


def prepare_kernel(ids_ref, gates_ref, rows_ref, gain_ref, out_ref):
    width = rows_ref.shape[1]
    rows = rows_ref[...].astype(f32)
    mean = jnp.mean(rows * rows, axis=1, keepdims=True)
    gain = gain_ref[...].astype(f32).reshape(1, width)
    out_ref[:, :width] = (rows * lax.rsqrt(mean + epsilon) * gain).astype(bf16)
    lane = lax.broadcasted_iota(jnp.int32, (1, 128), 1)
    expert, slot = lane // SLOTS, lane % SLOTS
    count = jnp.zeros((1, 128), jnp.int32)
    token = jnp.full((1, 128), -1.0, f32)
    gate = jnp.zeros((1, 128), f32)
    for t in range(TOK):
        picked = jnp.zeros((1, 128), jnp.int32)
        share = jnp.zeros((1, 128), f32)
        for j in range(8):
            hit = expert == ids_ref[t, j]
            picked = jnp.where(hit, 1, picked)
            share = share + jnp.where(hit, gates_ref[t, j], f32(0.0))
        here = (picked == 1) & (count == slot)
        token = jnp.where(here, f32(t), token)
        gate = jnp.where(here, share, gate)
        count = count + picked
    high = gate.astype(bf16).astype(f32)
    middle = (gate - high).astype(bf16).astype(f32)
    low = gate - high - middle
    row = lax.broadcasted_iota(jnp.int32, (TOK, 128), 0)
    facts = jnp.where(row == 0, token, jnp.where(row == 1, high, jnp.where(row == 2, middle, low)))
    out_ref[:, width:] = facts.astype(bf16)


def prepare(moe_rows, route_ids, route_gates, norm_gain):
    return pl.pallas_call(
        prepare_kernel,
        out_shape=jax.ShapeDtypeStruct((TOK, moe_rows.shape[1] + INFO), bf16),
        in_specs=[SMEM, SMEM, VMEM, VMEM],
        out_specs=VMEM,
    )(route_ids, route_gates, moe_rows, norm_gain)


def grid(rows, columns, dim):
    return lax.broadcasted_iota(jnp.int32, (rows, columns), dim)


def choose_kernel(place_ref, t0, t1, t2, t3, *out_refs):
    ctx, core, half, x, y = (place_ref[i] for i in range(5))
    width = out_refs[0].shape[1]
    refs = (t0, t1, t2, t3)
    facts = jnp.concatenate([ref[:, width:] for ref in refs], axis=0)
    first = grid(64, 64, 1) == grid(64, 64, 0) // TOK * TOK
    facts = jnp.dot(first.astype(f32).astype(bf16), facts, preferred_element_type=f32)
    row = grid(128, 128, 0)
    ahead = row // 32
    expert = jnp.where(core == 0, (x + ahead) % 4 * 4 + y, x * 4 + (y + ahead) % 4)
    lane = half * 32 + expert * SLOTS + row % SLOTS
    pick = (grid(128, 128, 1) == lane).astype(f32).astype(bf16)
    wanted = lax.dot_general(
        pick, facts.astype(bf16), (((1,), (1,)), ((), ())), preferred_element_type=f32
    )
    row, column = grid(128, 64, 0), grid(128, 64, 1)
    hit = wanted == (column % TOK).astype(f32)
    hit = hit & (column // 16 == row // 8 % 4)
    hit = hit & ((ctx - column // TOK % 4 + 4) % 4 == row // SLOTS % 4)
    selector = hit.astype(f32).astype(bf16)
    for low in range(0, width, STEP):
        tokens = jnp.concatenate([ref[:, low : low + STEP] for ref in refs], axis=0)
        part = jnp.dot(selector, tokens, preferred_element_type=f32).astype(bf16)
        for k, out_ref in enumerate(out_refs):
            out_ref[:, low : low + STEP] = part[32 * k : 32 * (k + 1)]


def choose(place, line, width):
    return pl.pallas_call(
        choose_kernel,
        out_shape=tuple(jax.ShapeDtypeStruct((32, width), bf16) for _ in range(4)),
        in_specs=[SMEM] + [VMEM] * 4,
        out_specs=(VMEM,) * 4,
        compiler_params=room(8),
        cost_estimate=pl.CostEstimate(flops=2 * 128 * 64 * width, bytes_accessed=2 * 192 * width, transcendentals=0),
    )(place, *line)


def gate_up_kernel(
    place_ref, r0, r1, r2, r3, own_hbm, other_hbm, out_ref, rows_ref, held_ref, hidden_ref, row_sems, sems
):
    core, x, y = place_ref[1], place_ref[3], place_ref[4]
    width = rows_ref.shape[1]
    moves = []
    for k, source in enumerate((r0, r1, r2, r3)):
        moves.append(pltpu.make_async_copy(source, rows_ref.at[pl.ds(32 * k, 32)], row_sems.at[k]))
        moves[k].start()
    copies = []
    for i in range(width // STEP):
        part = pl.ds(i * STEP, STEP)
        copies.append(
            [
                pltpu.make_async_copy(own_hbm.at[:, part], held_ref.at[0, :, part], sems.at[i, 0]),
                pltpu.make_async_copy(other_hbm.at[:, part], held_ref.at[1, :, part], sems.at[i, 1]),
            ]
        )
        for copy in copies[-1]:
            copy.start()
    sums = [jnp.zeros((128, 256), f32) for _ in range(4)]
    for move in moves:
        move.wait()
    for i in range(width // STEP):
        low, high = i * STEP, (i + 1) * STEP
        for copy in copies[i]:
            copy.wait()
        rows = rows_ref[:, low:high]
        for j in range(2):
            for k in range(2):
                sums[2 * j + k] += jnp.dot(rows, held_ref[j, k, low:high], preferred_element_type=f32)
    for j in range(2):
        gate, up = sums[2 * j], sums[2 * j + 1]
        hidden = gate / (1.0 + jnp.exp(-gate)) * up
        for v in range(4):
            for u in range(4):
                back_x = (x - jnp.where(core == 0, v, u) + 4) % 4
                back_y = (y - jnp.where(core == 0, u, v) + 4) % 4
                at = pl.ds(pl.multiple_of((back_x * 4 + back_y) * 8, 8), 8)
                low = 8 * (4 * v + u)
                hidden_ref[at, j * 256 : (j + 1) * 256] = hidden[low : low + 8]
    out_ref[...] = hidden_ref[...].astype(bf16)


def gate_up(place, rows, own, other):
    width = own.shape[1]
    return pl.pallas_call(
        gate_up_kernel,
        out_shape=jax.ShapeDtypeStruct((128, 512), bf16),
        in_specs=[SMEM] + [ANY] * 4 + [HBM] * 2,
        out_specs=VMEM,
        scratch_shapes=[
            pltpu.VMEM((128, width), bf16),
            pltpu.VMEM((2, 2, width, 256), bf16),
            pltpu.VMEM((128, 512), f32),
            pltpu.SemaphoreType.DMA((4,)),
            pltpu.SemaphoreType.DMA((width // STEP, 2)),
        ],
        compiler_params=room(46),
        cost_estimate=pl.CostEstimate(
            flops=2 * 128 * width * 1024, bytes_accessed=2 * width * (1024 + 128), transcendentals=65536
        ),
    )(place, *rows, own, other)


def down_kernel(place_ref, *refs):
    ctx, core = place_ref[0], place_ref[1]
    pieces, (own_hbm, other_hbm, out_ref, pieces_ref, held_ref, sems) = refs[:8], refs[8:]
    copies = []
    for k in range(4):
        source = (ctx - k + 4) % 4
        copies.append(
            [
                pltpu.make_async_copy(pieces[k], pieces_ref.at[k, pl.ds(0, 128)], sems.at[k, 0]),
                pltpu.make_async_copy(pieces[4 + k], pieces_ref.at[k, pl.ds(128, 128)], sems.at[k, 1]),
                pltpu.make_async_copy(own_hbm.at[source], held_ref.at[0, k], sems.at[k, 2]),
                pltpu.make_async_copy(other_hbm.at[source], held_ref.at[1, k], sems.at[k, 3]),
            ]
        )
        for copy in copies[-1]:
            copy.start()
    totals = [jnp.zeros((256, 896), f32) for _ in range(2)]
    for k in range(4):
        for copy in copies[k]:
            copy.wait()
        for j in range(2):
            totals[j] += jnp.dot(pieces_ref[k, :, :256], held_ref[j, k, core], preferred_element_type=f32)
            totals[j] += jnp.dot(pieces_ref[k, :, 256:], held_ref[j, k, 1 - core], preferred_element_type=f32)
    for j in range(2):
        total = jnp.where(core == j, totals[0], totals[1]).reshape(2, 16, 8, 896)
        total = jnp.concatenate([total[0], total[1]], axis=1).reshape(256, 896)
        out_ref[:, j * 896 : (j + 1) * 896] = total.astype(bf16)


def down(place, pieces, own, other):
    return pl.pallas_call(
        down_kernel,
        out_shape=jax.ShapeDtypeStruct((256, 1792), bf16),
        in_specs=[SMEM] + [ANY] * 8 + [HBM] * 2,
        out_specs=VMEM,
        scratch_shapes=[
            pltpu.VMEM((4, 256, 512), bf16),
            pltpu.VMEM((2, 4, 2, 256, 896), bf16),
            pltpu.SemaphoreType.DMA((4, 4)),
        ],
        compiler_params=room(53),
        cost_estimate=pl.CostEstimate(
            flops=2 * 256 * 2048 * 1792, bytes_accessed=2 * 2048 * 1792 + 2 * 256 * 2048, transcendentals=0
        ),
    )(place, *pieces, own, other)


def mix_kernel(place_ref, back, facts0, facts1, out_ref):
    ctx, half = place_ref[0], place_ref[2]
    lane = grid(128, 256, 1)
    spread = grid(128, 256, 0) == half * 32 + lane // 16 * SLOTS + lane % SLOTS
    spread = spread.astype(f32).astype(bf16)
    facts = jnp.concatenate([facts0[...], facts1[...]], axis=0)
    facts = jnp.dot(facts, spread, preferred_element_type=f32)
    at, lane = grid(32, 256, 0), grid(32, 256, 1)
    chunk, lane_ctx = lane // 8 % 2, lane // SLOTS % 4
    here = (at // 16 == chunk) & ((ctx - at // TOK % 4 + 4) % 4 == lane_ctx)
    token, high, middle, low = (
        jnp.sum(jnp.where(here & (at % TOK == i), facts, 0.0), axis=0, keepdims=True) for i in range(4)
    )
    fits = (at // 8 == lane_ctx) & (at // 4 % 2 == jnp.where(chunk == 0, half, 1 - half))
    fits = fits & ((at % TOK).astype(f32) == token)
    total = jnp.zeros((32, 1792), f32)
    for part in (high, middle, low):
        matrix = jnp.where(fits, part, 0.0).astype(bf16)
        total += jnp.dot(matrix, back[...], preferred_element_type=f32)
    out_ref[...] = total.reshape(8, TOK, 1792).astype(bf16)


def mix(place, back, facts0, facts1):
    return pl.pallas_call(
        mix_kernel,
        out_shape=jax.ShapeDtypeStruct((8, TOK, 1792), bf16),
        in_specs=[SMEM] + [VMEM] * 3,
        out_specs=VMEM,
        compiler_params=room(6),
        cost_estimate=pl.CostEstimate(flops=2 * 32 * 256 * 1792 * 3, bytes_accessed=1 << 20, transcendentals=0),
    )(place, back, facts0, facts1)


def shards(
    query_latent,
    query_rope,
    latent_cache,
    rope_keys,
    lengths,
    moe_rows,
    route_ids,
    route_gates,
    norm_gain,
    expert_in,
    expert_out,
):
    c = lax.axis_index("ctx")
    a = lax.axis_index("att")
    h = lax.axis_index("zhi")
    width = moe_rows.shape[1]
    swap_core = [(0, 1), (1, 0)]

    place = jnp.stack([c, a, h, lax.axis_index("x"), lax.axis_index("y")]).astype(jnp.int32)
    payload = prepare(moe_rows, route_ids, route_gates, norm_gain)

    def hop(value, k):
        return lax.ppermute(value, "ctx", [(i, (i + k) % 4) for i in range(4)])

    def along(value, k, second):
        pairs = []
        for i in range(32):
            core, x, y = i // 16, i // 4 % 4, i % 4
            if (core == 0) == second:
                x = (x + k) % 4
            else:
                y = (y + k) % 4
            pairs.append((i, core * 16 + x * 4 + y))
        return lax.ppermute(value, ("att", "x", "y"), pairs)

    def first_stage(tokens):
        return [tokens] + [along(tokens, k, False) for k in (1, 2, 3)]

    def second_stage(rows):
        return [rows[0]] + [along(rows[k], k, True) for k in (1, 2, 3)]

    def hidden_of(got):
        hidden = gate_up(place, got, weight_in, other_in)
        return [hidden] + [hop(hidden, k) for k in (1, 2, 3)]

    weight_in, weight_out = expert_in[0], expert_out[0].reshape(4, 2, 256, 896)
    payload, moving_in, moving_out = lax.optimization_barrier((payload, weight_in, weight_out))
    other_in = lax.ppermute(moving_in, "att", swap_core)
    other_out = lax.ppermute(moving_out, "att", swap_core)
    tokens0 = jnp.concatenate([payload] + [hop(payload, k) for k in (1, 2, 3)], axis=0)
    part = attend(query_latent, query_rope, latent_cache, rope_keys, lengths).reshape(4, 32, 640)
    tokens0, facts0, part = lax.optimization_barrier((tokens0, tokens0[:, width:], part))
    line0 = first_stage(tokens0)
    tokens1, line0[1] = lax.optimization_barrier((tokens0, line0[1]))
    tokens1 = lax.ppermute(tokens1, "zhi", swap_core)
    rows0 = choose(place, line0, width)
    got0 = second_stage(rows0)
    tokens1, facts1, got0[1] = lax.optimization_barrier((tokens1, tokens1[:, width:], got0[1]))
    line1 = first_stage(tokens1)
    pieces0 = hidden_of(got0)
    pieces0[0], *line1 = lax.optimization_barrier((pieces0[0], *line1))
    got1 = second_stage(choose(place, line1, width))

    pieces1 = hidden_of(got1)
    result = down(place, pieces0 + pieces1, weight_out, other_out)
    back = lax.all_to_all(result.reshape(16, 16, 1792), ("x", "y"), split_axis=0, concat_axis=0, tiled=True)
    part, _ = lax.optimization_barrier((part, result))
    parts = [lax.dynamic_index_in_dim(part, c, 0, keepdims=False)]
    for k in (1, 2, 3):
        sent = lax.dynamic_index_in_dim(part, (c + k) % 4, 0, keepdims=False)
        parts.append(hop(sent, k))
    attended = finish_attention(parts)

    outgoing = mix(place, back.reshape(256, 1792), facts0, facts1)
    final = lax.all_to_all(outgoing, ("ctx", "zhi"), split_axis=0, concat_axis=0, tiled=True)
    final = final.reshape(4, 2, TOK, 1792).astype(f32)
    routed = (final[:, 0] + final[:, 1]).transpose(1, 0, 2).reshape(TOK, 4 * 1792)
    return (attended, routed.astype(bf16))


def solution(mesh):
    fine = Mesh(mesh.devices.reshape(4, 2, 2, 4, 4), ("ctx", "att", "zhi", "x", "y"))
    exp = ("zhi", "x", "y")
    sequences = ("att",) + exp
    every = ("ctx", "att") + exp
    placed = (
        P(sequences, None, None),
        P(sequences, None, None),
        P(sequences, "ctx", None),
        P(sequences, None, "ctx"),
        P(sequences),
        P(every, None),
        P(every, None),
        P(every, None),
        P(),
        P(exp, None, None, ("ctx", "att")),
        P(exp, None, ("ctx", "att")),
    )
    return jax.shard_map(
        shards,
        mesh=fine,
        in_specs=placed,
        out_specs=(P(sequences, "ctx", None), P(every, None)),
        check_vma=False,
    )
```

```python
import jax
import jax.numpy as jnp
from jax import lax
from jax.experimental import pallas as pl
from jax.experimental.pallas import tpu as pltpu
from jax.sharding import Mesh, PartitionSpec as P

softmax_scale = 192.0 ** (-0.5)
epsilon = 1e-06
bf16 = jnp.bfloat16
f32 = jnp.float32
INFO = 128
TOK = 4
SLOTS = 2


def attend(query_latent, query_rope, latent_cache, rope_keys, lengths):
    shard_length = latent_cache.shape[1]
    first_position = lax.axis_index("ctx") * shard_length
    scores = jnp.einsum("hr,tr->ht", query_latent[0], latent_cache[0], preferred_element_type=f32)
    scores = scores + jnp.einsum("hp,pt->ht", query_rope[0], rope_keys[0], preferred_element_type=f32)
    position = first_position + jnp.arange(shard_length, dtype=jnp.int32)
    live_mask = position < lengths[0]
    weights = jnp.where(live_mask[None, :], jnp.exp(softmax_scale * scores), f32(0.0))
    mass = jnp.sum(weights, axis=1, keepdims=True)
    numerator = jnp.dot(weights.astype(bf16), latent_cache[0], preferred_element_type=f32)
    high = lax.reduce_precision(mass, 8, 7)
    low = mass - high
    tail = jnp.concatenate([jnp.broadcast_to(v, (128, 64)) for v in (high, low)], axis=1)
    return jnp.concatenate([numerator, tail], axis=1).astype(bf16)


def finish_attention(parts):
    summed = sum(v.astype(f32) for v in parts)
    return (summed[:, :512] / (summed[:, 512:513] + summed[:, 576:577])).astype(bf16)[None]


VMEM = pl.BlockSpec(memory_space=pltpu.VMEM)
SMEM = pl.BlockSpec(memory_space=pltpu.SMEM)
HBM = pl.BlockSpec(memory_space=pltpu.HBM)
ANY = pl.BlockSpec(memory_space=pl.ANY)
STEP = 1024


def room(mib):
    return pltpu.CompilerParams(vmem_limit_bytes=mib * 1024 * 1024)


def prepare_kernel(ids_ref, gates_ref, rows_ref, gain_ref, out_ref):
    width = rows_ref.shape[1]
    rows = rows_ref[...].astype(f32)
    mean = jnp.mean(rows * rows, axis=1, keepdims=True)
    gain = gain_ref[...].astype(f32).reshape(1, width)
    out_ref[:, :width] = (rows * lax.rsqrt(mean + epsilon) * gain).astype(bf16)
    lane = lax.broadcasted_iota(jnp.int32, (1, 128), 1)
    expert, slot = lane // SLOTS, lane % SLOTS
    count = jnp.zeros((1, 128), jnp.int32)
    token = jnp.full((1, 128), -1.0, f32)
    gate = jnp.zeros((1, 128), f32)
    for t in range(TOK):
        picked = jnp.zeros((1, 128), jnp.int32)
        share = jnp.zeros((1, 128), f32)
        for j in range(8):
            hit = expert == ids_ref[t, j]
            picked = jnp.where(hit, 1, picked)
            share = share + jnp.where(hit, gates_ref[t, j], f32(0.0))
        here = (picked == 1) & (count == slot)
        token = jnp.where(here, f32(t), token)
        gate = jnp.where(here, share, gate)
        count = count + picked
    high = gate.astype(bf16).astype(f32)
    middle = (gate - high).astype(bf16).astype(f32)
    low = gate - high - middle
    row = lax.broadcasted_iota(jnp.int32, (TOK, 128), 0)
    facts = jnp.where(row == 0, token, jnp.where(row == 1, high, jnp.where(row == 2, middle, low)))
    out_ref[:, width:] = facts.astype(bf16)


def prepare(moe_rows, route_ids, route_gates, norm_gain):
    return pl.pallas_call(
        prepare_kernel,
        out_shape=jax.ShapeDtypeStruct((TOK, moe_rows.shape[1] + INFO), bf16),
        in_specs=[SMEM, SMEM, VMEM, VMEM],
        out_specs=VMEM,
    )(route_ids, route_gates, moe_rows, norm_gain)


def grid(rows, columns, dim):
    return lax.broadcasted_iota(jnp.int32, (rows, columns), dim)


def choose_kernel(place_ref, t0, t1, t2, t3, *out_refs):
    ctx, core, half, x, y = (place_ref[i] for i in range(5))
    width = out_refs[0].shape[1]
    refs = (t0, t1, t2, t3)
    facts = jnp.concatenate([ref[:, width:] for ref in refs], axis=0)
    first = grid(64, 64, 1) == grid(64, 64, 0) // TOK * TOK
    facts = jnp.dot(first.astype(f32).astype(bf16), facts, preferred_element_type=f32)
    row = grid(128, 128, 0)
    ahead = row // 32
    expert = jnp.where(core == 0, (x + ahead) % 4 * 4 + y, x * 4 + (y + ahead) % 4)
    lane = half * 32 + expert * SLOTS + row % SLOTS
    pick = (grid(128, 128, 1) == lane).astype(f32).astype(bf16)
    wanted = lax.dot_general(
        pick, facts.astype(bf16), (((1,), (1,)), ((), ())), preferred_element_type=f32
    )
    row, column = grid(128, 64, 0), grid(128, 64, 1)
    hit = wanted == (column % TOK).astype(f32)
    hit = hit & (column // 16 == row // 8 % 4)
    hit = hit & ((ctx - column // TOK % 4 + 4) % 4 == row // SLOTS % 4)
    selector = hit.astype(f32).astype(bf16)
    for low in range(0, width, STEP):
        tokens = jnp.concatenate([ref[:, low : low + STEP] for ref in refs], axis=0)
        part = jnp.dot(selector, tokens, preferred_element_type=f32).astype(bf16)
        for k, out_ref in enumerate(out_refs):
            out_ref[:, low : low + STEP] = part[32 * k : 32 * (k + 1)]


def choose(place, line, width):
    return pl.pallas_call(
        choose_kernel,
        out_shape=tuple(jax.ShapeDtypeStruct((32, width), bf16) for _ in range(4)),
        in_specs=[SMEM] + [VMEM] * 4,
        out_specs=(VMEM,) * 4,
        compiler_params=room(8),
        cost_estimate=pl.CostEstimate(flops=2 * 128 * 64 * width, bytes_accessed=2 * 192 * width, transcendentals=0),
    )(place, *line)


def gate_up_kernel(
    place_ref, r0, r1, r2, r3, own_hbm, other_hbm, out_ref, rows_ref, held_ref, hidden_ref, row_sems, sems
):
    core, x, y = place_ref[1], place_ref[3], place_ref[4]
    width = rows_ref.shape[1]
    moves = []
    for k, source in enumerate((r0, r1, r2, r3)):
        moves.append(pltpu.make_async_copy(source, rows_ref.at[pl.ds(32 * k, 32)], row_sems.at[k]))
        moves[k].start()
    copies = []
    for i in range(width // STEP):
        part = pl.ds(i * STEP, STEP)
        copies.append(
            [
                pltpu.make_async_copy(own_hbm.at[:, part], held_ref.at[0, :, part], sems.at[i, 0]),
                pltpu.make_async_copy(other_hbm.at[:, part], held_ref.at[1, :, part], sems.at[i, 1]),
            ]
        )
        for copy in copies[-1]:
            copy.start()
    sums = [jnp.zeros((128, 256), f32) for _ in range(4)]
    for move in moves:
        move.wait()
    for i in range(width // STEP):
        low, high = i * STEP, (i + 1) * STEP
        for copy in copies[i]:
            copy.wait()
        rows = rows_ref[:, low:high]
        for j in range(2):
            for k in range(2):
                sums[2 * j + k] += jnp.dot(rows, held_ref[j, k, low:high], preferred_element_type=f32)
    for j in range(2):
        gate, up = sums[2 * j], sums[2 * j + 1]
        hidden = gate / (1.0 + jnp.exp(-gate)) * up
        for v in range(4):
            for u in range(4):
                back_x = (x - jnp.where(core == 0, v, u) + 4) % 4
                back_y = (y - jnp.where(core == 0, u, v) + 4) % 4
                at = pl.ds(pl.multiple_of((back_x * 4 + back_y) * 8, 8), 8)
                low = 8 * (4 * v + u)
                hidden_ref[at, j * 256 : (j + 1) * 256] = hidden[low : low + 8]
    out_ref[...] = hidden_ref[...].astype(bf16)


def gate_up(place, rows, own, other):
    width = own.shape[1]
    return pl.pallas_call(
        gate_up_kernel,
        out_shape=jax.ShapeDtypeStruct((128, 512), bf16),
        in_specs=[SMEM] + [ANY] * 4 + [HBM] * 2,
        out_specs=VMEM,
        scratch_shapes=[
            pltpu.VMEM((128, width), bf16),
            pltpu.VMEM((2, 2, width, 256), bf16),
            pltpu.VMEM((128, 512), f32),
            pltpu.SemaphoreType.DMA((4,)),
            pltpu.SemaphoreType.DMA((width // STEP, 2)),
        ],
        compiler_params=room(46),
        cost_estimate=pl.CostEstimate(
            flops=2 * 128 * width * 1024, bytes_accessed=2 * width * (1024 + 128), transcendentals=65536
        ),
    )(place, *rows, own, other)


def down_kernel(place_ref, *refs):
    ctx, core = place_ref[0], place_ref[1]
    pieces, (own_hbm, other_hbm, out_ref, pieces_ref, held_ref, sems) = refs[:8], refs[8:]
    copies = []
    for k in range(4):
        source = (ctx - k + 4) % 4
        copies.append(
            [
                pltpu.make_async_copy(pieces[k], pieces_ref.at[k, pl.ds(0, 128)], sems.at[k, 0]),
                pltpu.make_async_copy(pieces[4 + k], pieces_ref.at[k, pl.ds(128, 128)], sems.at[k, 1]),
                pltpu.make_async_copy(own_hbm.at[source], held_ref.at[0, k], sems.at[k, 2]),
                pltpu.make_async_copy(other_hbm.at[source], held_ref.at[1, k], sems.at[k, 3]),
            ]
        )
        for copy in copies[-1]:
            copy.start()
    totals = [jnp.zeros((256, 896), f32) for _ in range(2)]
    for k in range(4):
        for copy in copies[k]:
            copy.wait()
        for j in range(2):
            totals[j] += jnp.dot(pieces_ref[k, :, :256], held_ref[j, k, core], preferred_element_type=f32)
            totals[j] += jnp.dot(pieces_ref[k, :, 256:], held_ref[j, k, 1 - core], preferred_element_type=f32)
    for j in range(2):
        total = jnp.where(core == j, totals[0], totals[1]).reshape(2, 16, 8, 896)
        total = jnp.concatenate([total[0], total[1]], axis=1).reshape(256, 896)
        out_ref[:, j * 896 : (j + 1) * 896] = total.astype(bf16)


def down(place, pieces, own, other):
    return pl.pallas_call(
        down_kernel,
        out_shape=jax.ShapeDtypeStruct((256, 1792), bf16),
        in_specs=[SMEM] + [ANY] * 8 + [HBM] * 2,
        out_specs=VMEM,
        scratch_shapes=[
            pltpu.VMEM((4, 256, 512), bf16),
            pltpu.VMEM((2, 4, 2, 256, 896), bf16),
            pltpu.SemaphoreType.DMA((4, 4)),
        ],
        compiler_params=room(53),
        cost_estimate=pl.CostEstimate(
            flops=2 * 256 * 2048 * 1792, bytes_accessed=2 * 2048 * 1792 + 2 * 256 * 2048, transcendentals=0
        ),
    )(place, *pieces, own, other)


def weigh_kernel(place_ref, facts0, facts1, out_ref):
    ctx, half = place_ref[0], place_ref[2]
    lane = grid(128, 256, 1)
    spread = grid(128, 256, 0) == half * 32 + lane // 16 * SLOTS + lane % SLOTS
    spread = spread.astype(f32).astype(bf16)
    facts = jnp.concatenate([facts0[...], facts1[...]], axis=0)
    facts = jnp.dot(facts, spread, preferred_element_type=f32)
    at, lane = grid(32, 256, 0), grid(32, 256, 1)
    chunk, lane_ctx = lane // 8 % 2, lane // SLOTS % 4
    here = (at // 16 == chunk) & ((ctx - at // TOK % 4 + 4) % 4 == lane_ctx)
    token, high, middle, low = (
        jnp.sum(jnp.where(here & (at % TOK == i), facts, 0.0), axis=0, keepdims=True) for i in range(4)
    )
    fits = (at // 8 == lane_ctx) & (at // 4 % 2 == jnp.where(chunk == 0, half, 1 - half))
    fits = fits & ((at % TOK).astype(f32) == token)
    for i, part in enumerate((high, middle, low)):
        out_ref[32 * i : 32 * (i + 1)] = jnp.where(fits, part, 0.0).astype(bf16)


def weigh(place, facts0, facts1):
    return pl.pallas_call(
        weigh_kernel,
        out_shape=jax.ShapeDtypeStruct((96, 256), bf16),
        in_specs=[SMEM] + [VMEM] * 2,
        out_specs=VMEM,
        compiler_params=room(6),
        cost_estimate=pl.CostEstimate(flops=1 << 22, bytes_accessed=1 << 17, transcendentals=0),
    )(place, facts0, facts1)


def mix_kernel(gates, back, out_ref):
    parts = jnp.dot(gates[...], back[...], preferred_element_type=f32)
    total = parts[:32] + parts[32:64] + parts[64:]
    out_ref[...] = total.reshape(8, TOK, 1792).astype(bf16)


def mix(gates, back):
    return pl.pallas_call(
        mix_kernel,
        out_shape=jax.ShapeDtypeStruct((8, TOK, 1792), bf16),
        in_specs=[VMEM] * 2,
        out_specs=VMEM,
        compiler_params=room(6),
        cost_estimate=pl.CostEstimate(flops=2 * 96 * 256 * 1792, bytes_accessed=1 << 20, transcendentals=0),
    )(gates, back)


def shards(
    query_latent,
    query_rope,
    latent_cache,
    rope_keys,
    lengths,
    moe_rows,
    route_ids,
    route_gates,
    norm_gain,
    expert_in,
    expert_out,
):
    c = lax.axis_index("ctx")
    a = lax.axis_index("att")
    h = lax.axis_index("zhi")
    width = moe_rows.shape[1]
    swap_core = [(0, 1), (1, 0)]

    place = jnp.stack([c, a, h, lax.axis_index("x"), lax.axis_index("y")]).astype(jnp.int32)
    payload = prepare(moe_rows, route_ids, route_gates, norm_gain)

    def hop(value, k):
        return lax.ppermute(value, "ctx", [(i, (i + k) % 4) for i in range(4)])

    def along(value, k, second):
        pairs = []
        for i in range(32):
            core, x, y = i // 16, i // 4 % 4, i % 4
            if (core == 0) == second:
                x = (x + k) % 4
            else:
                y = (y + k) % 4
            pairs.append((i, core * 16 + x * 4 + y))
        return lax.ppermute(value, ("att", "x", "y"), pairs)

    def first_stage(tokens):
        return [tokens] + [along(tokens, k, False) for k in (1, 2, 3)]

    def second_stage(rows):
        return [rows[0]] + [along(rows[k], k, True) for k in (1, 2, 3)]

    def hidden_of(got):
        hidden = gate_up(place, got, weight_in, other_in)
        return [hidden] + [hop(hidden, k) for k in (1, 2, 3)]

    weight_in, weight_out = expert_in[0], expert_out[0].reshape(4, 2, 256, 896)
    payload, moving_in, moving_out = lax.optimization_barrier((payload, weight_in, weight_out))
    other_in = lax.ppermute(moving_in, "att", swap_core)
    other_out = lax.ppermute(moving_out, "att", swap_core)
    tokens0 = jnp.concatenate([payload] + [hop(payload, k) for k in (1, 2, 3)], axis=0)
    part = attend(query_latent, query_rope, latent_cache, rope_keys, lengths).reshape(4, 32, 640)
    tokens0, facts0, part = lax.optimization_barrier((tokens0, tokens0[:, width:], part))
    line0 = first_stage(tokens0)
    tokens1, line0[1] = lax.optimization_barrier((tokens0, line0[1]))
    tokens1 = lax.ppermute(tokens1, "zhi", swap_core)
    rows0 = choose(place, line0, width)
    got0 = second_stage(rows0)
    tokens1, facts1, got0[1] = lax.optimization_barrier((tokens1, tokens1[:, width:], got0[1]))
    line1 = first_stage(tokens1)
    pieces0 = hidden_of(got0)
    pieces0[0], *line1 = lax.optimization_barrier((pieces0[0], *line1))
    got1 = second_stage(choose(place, line1, width))

    pieces1 = hidden_of(got1)
    result = down(place, pieces0 + pieces1, weight_out, other_out)
    back = lax.all_to_all(result.reshape(16, 16, 1792), ("x", "y"), split_axis=0, concat_axis=0, tiled=True)
    part, facts0, facts1, _ = lax.optimization_barrier((part, facts0, facts1, result))
    gates = weigh(place, facts0, facts1)
    parts = [lax.dynamic_index_in_dim(part, c, 0, keepdims=False)]
    for k in (1, 2, 3):
        sent = lax.dynamic_index_in_dim(part, (c + k) % 4, 0, keepdims=False)
        parts.append(hop(sent, k))
    attended = finish_attention(parts)

    outgoing = mix(gates, back.reshape(256, 1792))
    final = lax.all_to_all(outgoing, ("ctx", "zhi"), split_axis=0, concat_axis=0, tiled=True)
    final = final.reshape(4, 2, TOK, 1792).astype(f32)
    routed = (final[:, 0] + final[:, 1]).transpose(1, 0, 2).reshape(TOK, 4 * 1792)
    return (attended, routed.astype(bf16))


def solution(mesh):
    fine = Mesh(mesh.devices.reshape(4, 2, 2, 4, 4), ("ctx", "att", "zhi", "x", "y"))
    exp = ("zhi", "x", "y")
    sequences = ("att",) + exp
    every = ("ctx", "att") + exp
    placed = (
        P(sequences, None, None),
        P(sequences, None, None),
        P(sequences, "ctx", None),
        P(sequences, None, "ctx"),
        P(sequences),
        P(every, None),
        P(every, None),
        P(every, None),
        P(),
        P(exp, None, None, ("ctx", "att")),
        P(exp, None, ("ctx", "att")),
    )
    return jax.shard_map(
        shards,
        mesh=fine,
        in_specs=placed,
        out_specs=(P(sequences, "ctx", None), P(every, None)),
        check_vma=False,
    )
```

```python
import jax
import jax.numpy as jnp
from jax import lax
from jax.experimental import pallas as pl
from jax.experimental.pallas import tpu as pltpu
from jax.sharding import Mesh, PartitionSpec as P

softmax_scale = 192.0 ** (-0.5)
epsilon = 1e-06
bf16 = jnp.bfloat16
f32 = jnp.float32
INFO = 128
TOK = 4
SLOTS = 2


def attend(query_latent, query_rope, latent_cache, rope_keys, lengths):
    shard_length = latent_cache.shape[1]
    first_position = lax.axis_index("ctx") * shard_length
    scores = jnp.einsum("hr,tr->ht", query_latent[0], latent_cache[0], preferred_element_type=f32)
    scores = scores + jnp.einsum("hp,pt->ht", query_rope[0], rope_keys[0], preferred_element_type=f32)
    position = first_position + jnp.arange(shard_length, dtype=jnp.int32)
    live_mask = position < lengths[0]
    weights = jnp.where(live_mask[None, :], jnp.exp(softmax_scale * scores), f32(0.0))
    mass = jnp.sum(weights, axis=1, keepdims=True)
    numerator = jnp.dot(weights.astype(bf16), latent_cache[0], preferred_element_type=f32)
    high = lax.reduce_precision(mass, 8, 7)
    low = mass - high
    tail = jnp.concatenate([jnp.broadcast_to(v, (128, 64)) for v in (high, low)], axis=1)
    return jnp.concatenate([numerator, tail], axis=1).astype(bf16)


def finish_attention(parts):
    summed = sum(v.astype(f32) for v in parts)
    return (summed[:, :512] / (summed[:, 512:513] + summed[:, 576:577])).astype(bf16)[None]


VMEM = pl.BlockSpec(memory_space=pltpu.VMEM)
SMEM = pl.BlockSpec(memory_space=pltpu.SMEM)
HBM = pl.BlockSpec(memory_space=pltpu.HBM)
ANY = pl.BlockSpec(memory_space=pl.ANY)
STEP = 1024


def room(mib):
    return pltpu.CompilerParams(vmem_limit_bytes=mib * 1024 * 1024)


def prepare_kernel(ids_ref, gates_ref, rows_ref, gain_ref, out_ref):
    width = rows_ref.shape[1]
    rows = rows_ref[...].astype(f32)
    mean = jnp.mean(rows * rows, axis=1, keepdims=True)
    gain = gain_ref[...].astype(f32).reshape(1, width)
    out_ref[:, :width] = (rows * lax.rsqrt(mean + epsilon) * gain).astype(bf16)
    lane = lax.broadcasted_iota(jnp.int32, (1, 128), 1)
    expert, slot = lane // SLOTS, lane % SLOTS
    count = jnp.zeros((1, 128), jnp.int32)
    token = jnp.full((1, 128), -1.0, f32)
    gate = jnp.zeros((1, 128), f32)
    for t in range(TOK):
        picked = jnp.zeros((1, 128), jnp.int32)
        share = jnp.zeros((1, 128), f32)
        for j in range(8):
            hit = expert == ids_ref[t, j]
            picked = jnp.where(hit, 1, picked)
            share = share + jnp.where(hit, gates_ref[t, j], f32(0.0))
        here = (picked == 1) & (count == slot)
        token = jnp.where(here, f32(t), token)
        gate = jnp.where(here, share, gate)
        count = count + picked
    high = gate.astype(bf16).astype(f32)
    middle = (gate - high).astype(bf16).astype(f32)
    low = gate - high - middle
    row = lax.broadcasted_iota(jnp.int32, (TOK, 128), 0)
    facts = jnp.where(row == 0, token, jnp.where(row == 1, high, jnp.where(row == 2, middle, low)))
    out_ref[:, width:] = facts.astype(bf16)


def prepare(moe_rows, route_ids, route_gates, norm_gain):
    return pl.pallas_call(
        prepare_kernel,
        out_shape=jax.ShapeDtypeStruct((TOK, moe_rows.shape[1] + INFO), bf16),
        in_specs=[SMEM, SMEM, VMEM, VMEM],
        out_specs=VMEM,
    )(route_ids, route_gates, moe_rows, norm_gain)


def grid(rows, columns, dim):
    return lax.broadcasted_iota(jnp.int32, (rows, columns), dim)


def choose_kernel(place_ref, t0, t1, t2, t3, *out_refs):
    ctx, core, half, x, y = (place_ref[i] for i in range(5))
    width = out_refs[0].shape[1]
    refs = (t0, t1, t2, t3)
    facts = jnp.concatenate([ref[:, width:] for ref in refs], axis=0)
    first = grid(64, 64, 1) == grid(64, 64, 0) // TOK * TOK
    facts = jnp.dot(first.astype(f32).astype(bf16), facts, preferred_element_type=f32)
    row = grid(128, 128, 0)
    ahead = row // 32
    expert = jnp.where(core == 0, (x + ahead) % 4 * 4 + y, x * 4 + (y + ahead) % 4)
    lane = half * 32 + expert * SLOTS + row % SLOTS
    pick = (grid(128, 128, 1) == lane).astype(f32).astype(bf16)
    wanted = lax.dot_general(
        pick, facts.astype(bf16), (((1,), (1,)), ((), ())), preferred_element_type=f32
    )
    row, column = grid(128, 64, 0), grid(128, 64, 1)
    hit = wanted == (column % TOK).astype(f32)
    hit = hit & (column // 16 == row // 8 % 4)
    hit = hit & ((ctx - column // TOK % 4 + 4) % 4 == row // SLOTS % 4)
    selector = hit.astype(f32).astype(bf16)
    for low in range(0, width, STEP):
        tokens = jnp.concatenate([ref[:, low : low + STEP] for ref in refs], axis=0)
        part = jnp.dot(selector, tokens, preferred_element_type=f32).astype(bf16)
        for k, out_ref in enumerate(out_refs):
            out_ref[:, low : low + STEP] = part[32 * k : 32 * (k + 1)]


def choose(place, line, width):
    return pl.pallas_call(
        choose_kernel,
        out_shape=tuple(jax.ShapeDtypeStruct((32, width), bf16) for _ in range(4)),
        in_specs=[SMEM] + [VMEM] * 4,
        out_specs=(VMEM,) * 4,
        compiler_params=room(8),
        cost_estimate=pl.CostEstimate(flops=2 * 128 * 64 * width, bytes_accessed=2 * 192 * width, transcendentals=0),
    )(place, *line)


def gate_up_kernel(
    place_ref, r0, r1, r2, r3, own_hbm, other_hbm, out_ref, rows_ref, held_ref, hidden_ref, row_sems, sems
):
    core, x, y = place_ref[1], place_ref[3], place_ref[4]
    width = rows_ref.shape[1]
    moves = []
    for k, source in enumerate((r0, r1, r2, r3)):
        moves.append(pltpu.make_async_copy(source, rows_ref.at[pl.ds(32 * k, 32)], row_sems.at[k]))
        moves[k].start()
    copies = []
    for i in range(width // STEP):
        part = pl.ds(i * STEP, STEP)
        copies.append(
            [
                pltpu.make_async_copy(own_hbm.at[:, part], held_ref.at[0, :, part], sems.at[i, 0]),
                pltpu.make_async_copy(other_hbm.at[:, part], held_ref.at[1, :, part], sems.at[i, 1]),
            ]
        )
        for copy in copies[-1]:
            copy.start()
    sums = [jnp.zeros((128, 256), f32) for _ in range(4)]
    for move in moves:
        move.wait()
    for i in range(width // STEP):
        low, high = i * STEP, (i + 1) * STEP
        for copy in copies[i]:
            copy.wait()
        rows = rows_ref[:, low:high]
        for j in range(2):
            for k in range(2):
                sums[2 * j + k] += jnp.dot(rows, held_ref[j, k, low:high], preferred_element_type=f32)
    for j in range(2):
        gate, up = sums[2 * j], sums[2 * j + 1]
        hidden = gate / (1.0 + jnp.exp(-gate)) * up
        for v in range(4):
            for u in range(4):
                back_x = (x - jnp.where(core == 0, v, u) + 4) % 4
                back_y = (y - jnp.where(core == 0, u, v) + 4) % 4
                at = pl.ds(pl.multiple_of((back_x * 4 + back_y) * 8, 8), 8)
                low = 8 * (4 * v + u)
                hidden_ref[at, j * 256 : (j + 1) * 256] = hidden[low : low + 8]
    out_ref[...] = hidden_ref[...].astype(bf16)


def gate_up(place, rows, own, other):
    width = own.shape[1]
    return pl.pallas_call(
        gate_up_kernel,
        out_shape=jax.ShapeDtypeStruct((128, 512), bf16),
        in_specs=[SMEM] + [ANY] * 4 + [HBM] * 2,
        out_specs=VMEM,
        scratch_shapes=[
            pltpu.VMEM((128, width), bf16),
            pltpu.VMEM((2, 2, width, 256), bf16),
            pltpu.VMEM((128, 512), f32),
            pltpu.SemaphoreType.DMA((4,)),
            pltpu.SemaphoreType.DMA((width // STEP, 2)),
        ],
        compiler_params=room(46),
        cost_estimate=pl.CostEstimate(
            flops=2 * 128 * width * 1024, bytes_accessed=2 * width * (1024 + 128), transcendentals=65536
        ),
    )(place, *rows, own, other)


def down_kernel(place_ref, *refs):
    ctx, core = place_ref[0], place_ref[1]
    pieces, (own_hbm, other_hbm, out_ref, pieces_ref, held_ref, sems) = refs[:8], refs[8:]
    copies = []
    for k in range(4):
        source = (ctx - k + 4) % 4
        copies.append(
            [
                pltpu.make_async_copy(pieces[k], pieces_ref.at[k, pl.ds(0, 128)], sems.at[k, 0]),
                pltpu.make_async_copy(pieces[4 + k], pieces_ref.at[k, pl.ds(128, 128)], sems.at[k, 1]),
                pltpu.make_async_copy(own_hbm.at[source], held_ref.at[0, k], sems.at[k, 2]),
                pltpu.make_async_copy(other_hbm.at[source], held_ref.at[1, k], sems.at[k, 3]),
            ]
        )
        for copy in copies[-1]:
            copy.start()
    totals = [jnp.zeros((256, 896), f32) for _ in range(2)]
    for k in range(4):
        for copy in copies[k]:
            copy.wait()
        for j in range(2):
            totals[j] += jnp.dot(pieces_ref[k, :, :256], held_ref[j, k, core], preferred_element_type=f32)
            totals[j] += jnp.dot(pieces_ref[k, :, 256:], held_ref[j, k, 1 - core], preferred_element_type=f32)
    for j in range(2):
        total = jnp.where(core == j, totals[0], totals[1]).reshape(2, 16, 8, 896)
        total = jnp.concatenate([total[0], total[1]], axis=1).reshape(256, 896)
        out_ref[:, j * 896 : (j + 1) * 896] = total.astype(bf16)


def down(place, pieces, own, other):
    return pl.pallas_call(
        down_kernel,
        out_shape=jax.ShapeDtypeStruct((256, 1792), bf16),
        in_specs=[SMEM] + [ANY] * 8 + [HBM] * 2,
        out_specs=VMEM,
        scratch_shapes=[
            pltpu.VMEM((4, 256, 512), bf16),
            pltpu.VMEM((2, 4, 2, 256, 896), bf16),
            pltpu.SemaphoreType.DMA((4, 4)),
        ],
        compiler_params=room(51),
        cost_estimate=pl.CostEstimate(
            flops=2 * 256 * 2048 * 1792, bytes_accessed=2 * 2048 * 1792 + 2 * 256 * 2048, transcendentals=0
        ),
    )(place, *pieces, own, other)


def weigh_kernel(place_ref, facts0, facts1, out_ref):
    ctx, half = place_ref[0], place_ref[2]
    lane = grid(128, 256, 1)
    spread = grid(128, 256, 0) == half * 32 + lane // 16 * SLOTS + lane % SLOTS
    spread = spread.astype(f32).astype(bf16)
    facts = jnp.concatenate([facts0[...], facts1[...]], axis=0)
    facts = jnp.dot(facts, spread, preferred_element_type=f32)
    at, lane = grid(32, 256, 0), grid(32, 256, 1)
    chunk, lane_ctx = lane // 8 % 2, lane // SLOTS % 4
    here = (at // 16 == chunk) & ((ctx - at // TOK % 4 + 4) % 4 == lane_ctx)
    token, high, middle, low = (
        jnp.sum(jnp.where(here & (at % TOK == i), facts, 0.0), axis=0, keepdims=True) for i in range(4)
    )
    fits = (at // 8 == lane_ctx) & (at // 4 % 2 == jnp.where(chunk == 0, half, 1 - half))
    fits = fits & ((at % TOK).astype(f32) == token)
    for i, part in enumerate((high, middle, low)):
        out_ref[32 * i : 32 * (i + 1)] = jnp.where(fits, part, 0.0).astype(bf16)


def weigh(place, facts0, facts1):
    return pl.pallas_call(
        weigh_kernel,
        out_shape=jax.ShapeDtypeStruct((96, 256), bf16),
        in_specs=[SMEM] + [VMEM] * 2,
        out_specs=VMEM,
        compiler_params=room(6),
        cost_estimate=pl.CostEstimate(flops=1 << 22, bytes_accessed=1 << 17, transcendentals=0),
    )(place, facts0, facts1)


def mix_kernel(gates, back, out_ref):
    parts = jnp.dot(gates[...], back[...], preferred_element_type=f32)
    total = parts[:32] + parts[32:64] + parts[64:]
    out_ref[...] = total.reshape(8, TOK, 1792).astype(bf16)


def mix(gates, back):
    return pl.pallas_call(
        mix_kernel,
        out_shape=jax.ShapeDtypeStruct((8, TOK, 1792), bf16),
        in_specs=[VMEM] * 2,
        out_specs=VMEM,
        compiler_params=room(6),
        cost_estimate=pl.CostEstimate(flops=2 * 96 * 256 * 1792, bytes_accessed=1 << 20, transcendentals=0),
    )(gates, back)


def shards(
    query_latent,
    query_rope,
    latent_cache,
    rope_keys,
    lengths,
    moe_rows,
    route_ids,
    route_gates,
    norm_gain,
    expert_in,
    expert_out,
):
    c = lax.axis_index("ctx")
    a = lax.axis_index("att")
    h = lax.axis_index("zhi")
    width = moe_rows.shape[1]
    swap_core = [(0, 1), (1, 0)]

    place = jnp.stack([c, a, h, lax.axis_index("x"), lax.axis_index("y")]).astype(jnp.int32)
    payload = prepare(moe_rows, route_ids, route_gates, norm_gain)

    def hop(value, k):
        return lax.ppermute(value, "ctx", [(i, (i + k) % 4) for i in range(4)])

    def along(value, k, second):
        pairs = []
        for i in range(32):
            core, x, y = i // 16, i // 4 % 4, i % 4
            if (core == 0) == second:
                x = (x + k) % 4
            else:
                y = (y + k) % 4
            pairs.append((i, core * 16 + x * 4 + y))
        return lax.ppermute(value, ("att", "x", "y"), pairs)

    def first_stage(tokens):
        return [tokens] + [along(tokens, k, False) for k in (1, 2, 3)]

    def second_stage(rows):
        return [rows[0]] + [along(rows[k], k, True) for k in (1, 2, 3)]

    def hidden_of(got):
        hidden = gate_up(place, got, weight_in, other_in)
        return [hidden] + [hop(hidden, k) for k in (1, 2, 3)]

    weight_in, weight_out = expert_in[0], expert_out[0].reshape(4, 2, 256, 896)
    payload, moving_in, moving_out = lax.optimization_barrier((payload, weight_in, weight_out))
    other_in = lax.ppermute(moving_in, "att", swap_core)
    other_out = lax.ppermute(moving_out, "att", swap_core)
    tokens0 = jnp.concatenate([payload] + [hop(payload, k) for k in (1, 2, 3)], axis=0)
    part = attend(query_latent, query_rope, latent_cache, rope_keys, lengths).reshape(4, 32, 640)
    tokens0, facts0, part = lax.optimization_barrier((tokens0, tokens0[:, width:], part))
    line0 = first_stage(tokens0)
    tokens1, line0[1] = lax.optimization_barrier((tokens0, line0[1]))
    tokens1 = lax.ppermute(tokens1, "zhi", swap_core)
    rows0 = choose(place, line0, width)
    got0 = second_stage(rows0)
    tokens1, facts1, got0[1] = lax.optimization_barrier((tokens1, tokens1[:, width:], got0[1]))
    line1 = first_stage(tokens1)
    pieces0 = hidden_of(got0)
    pieces0[0], *line1 = lax.optimization_barrier((pieces0[0], *line1))
    got1 = second_stage(choose(place, line1, width))

    pieces1 = hidden_of(got1)
    result = down(place, pieces0 + pieces1, weight_out, other_out)
    back = lax.all_to_all(result.reshape(16, 16, 1792), ("x", "y"), split_axis=0, concat_axis=0, tiled=True)
    part, facts0, facts1, _ = lax.optimization_barrier((part, facts0, facts1, result))
    gates = weigh(place, facts0, facts1)
    parts = [lax.dynamic_index_in_dim(part, c, 0, keepdims=False)]
    for k in (1, 2, 3):
        sent = lax.dynamic_index_in_dim(part, (c + k) % 4, 0, keepdims=False)
        parts.append(hop(sent, k))
    attended = finish_attention(parts)

    outgoing = mix(gates, back.reshape(256, 1792))
    final = lax.all_to_all(outgoing, ("ctx", "zhi"), split_axis=0, concat_axis=0, tiled=True)
    final = final.reshape(4, 2, TOK, 1792).astype(f32)
    routed = (final[:, 0] + final[:, 1]).transpose(1, 0, 2).reshape(TOK, 4 * 1792)
    return (attended, routed.astype(bf16))


def solution(mesh):
    fine = Mesh(mesh.devices.reshape(4, 2, 2, 4, 4), ("ctx", "att", "zhi", "x", "y"))
    exp = ("zhi", "x", "y")
    sequences = ("att",) + exp
    every = ("ctx", "att") + exp
    placed = (
        P(sequences, None, None),
        P(sequences, None, None),
        P(sequences, "ctx", None),
        P(sequences, None, "ctx"),
        P(sequences),
        P(every, None),
        P(every, None),
        P(every, None),
        P(),
        P(exp, None, None, ("ctx", "att")),
        P(exp, None, ("ctx", "att")),
    )
    return jax.shard_map(
        shards,
        mesh=fine,
        in_specs=placed,
        out_specs=(P(sequences, "ctx", None), P(every, None)),
        check_vma=False,
    )
```
